512 devices in a mesh: occ: 16 (over x, z_lo, core), vir: 32 (over z_hi, y).
Axes of the slice: x: 4, y: 8, z: 8 (z_hi: 4, z_lo: 2; z = z_hi * 2 + z_lo), core: 2. Of those that a mesh axis runs over, the one named last changes fastest.
Arguments:
- amplitudes: float32 [64, 64, 1024], P('occ'), may hold values from -6 to 6
- integrals: float32 [256, 256, 1024], P('vir', 'occ'), may hold values from -0.53033006 to 0.53033006
- occ_energy: float32 [64], replicated, may hold values from -2 to -0.5
- vir_energy: float32 [256], replicated, may hold values from 0.5 to 3
- occ_irrep: int32 [64], replicated, may hold values from 0 to 7
- vir_irrep: int32 [256], replicated, may hold values from 0 to 7
- pair_irrep: int32 [1024], replicated, may hold values from 0 to 7
Outputs:
- update: float32 [64, 64, 256, 256], P('occ', None, 'vir')
The draws below stay inside these ranges and needn't reach their ends.
All inputs are finite; a program needn't handle non-finite values.
Results may differ from the reference program's by a relative error of at most 0.00007.
Values sent between devices are 32-bit elements; how exact they have to be, the bound alone decides.
A program may use at most 128 MiB of HBM per device.

```python
import jax
import jax.numpy as jnp
from jax import lax

NO = 64
NV = 256
CD = 1024


def with_ends(values, stream_key, smallest, high):
    extent = values.shape
    spot = [jax.random.randint(jax.random.fold_in(stream_key, axis), (), 0, extent[axis]) for axis in range(len(extent))]
    values = values.at[tuple(spot)].set(smallest)
    longest = extent.index(max(extent))
    spot[longest] = (spot[longest] + 1) % extent[longest]
    return values.at[tuple(spot)].set(high)


def level_of(rng, extent, pieces, least, high):
    loudness = 1.0
    for position, shards_of in pieces:
        steps = jax.random.uniform(jax.random.fold_in(jax.random.fold_in(rng, 6), position), (shards_of,), jnp.float32, least / len(pieces), high / len(pieces))
        loudness = loudness * jnp.repeat(jnp.exp(steps), extent[position] // shards_of).reshape((-1,) + (1,) * (len(extent) - 1 - position))
    return loudness


def normal_values(rng, dims, width, bound, cuts=(), dtype=jnp.bfloat16):
    result = jax.random.normal(rng, dims, jnp.float32) * width
    if len(cuts) > 0:
        result = level_of(rng, dims, cuts, -0.22, 0.18) * result
    return jnp.clip(result, min=-bound, max=bound).astype(dtype)


def setup_inputs(seed: int = 0) -> dict:
    keys = jax.random.split(jax.random.key(seed), 8)
    amplitudes = normal_values(keys[0], (NO, NO, CD), 1.0, 6.0, ((0, 16),), jnp.float32)
    integrals = normal_values(keys[1], (NV, NV, CD), ((8.0 / CD) ** 0.5), 0.53033006, ((0, 32), (1, 16)), jnp.float32)
    occ_energy = jnp.clip(jax.random.uniform(keys[2], (NO,), jnp.float32, -2.0, -0.5), -2.0, -0.5)
    vir_energy = jnp.clip(jax.random.uniform(keys[3], (NV,), jnp.float32, 0.5, 3.0), 0.5, 3.0)
    occ_irrep = with_ends(jax.random.randint(keys[4], (NO,), 0, 8), jax.random.fold_in(keys[4], 1), 0, 7).astype(jnp.int32)
    vir_irrep = with_ends(jax.random.randint(keys[5], (NV,), 0, 8), jax.random.fold_in(keys[5], 1), 0, 7).astype(jnp.int32)
    pair_irrep = with_ends(jax.random.randint(keys[6], (CD,), 0, 8), jax.random.fold_in(keys[6], 1), 0, 7).astype(jnp.int32)
    return {"amplitudes": amplitudes, "integrals": integrals, "occ_energy": occ_energy, "vir_energy": vir_energy, "occ_irrep": occ_irrep, "vir_irrep": vir_irrep, "pair_irrep": pair_irrep}


def reference(amplitudes, integrals, occ_energy, vir_energy, occ_irrep, vir_irrep, pair_irrep):
    pair_sym = jnp.bitwise_xor(occ_irrep[:, None], occ_irrep[None, :])
    masked_amp = jnp.where(pair_sym[:, :, None] == pair_irrep[None, None, :], amplitudes, jnp.float32(0.0))
    vir_sym = jnp.bitwise_xor(vir_irrep[:, None], vir_irrep[None, :])
    masked_int = jnp.where(vir_sym[:, :, None] == pair_irrep[None, None, :], integrals, jnp.float32(0.0))

    def one_row(row):
        return jnp.einsum("ijk,bk->ijb", masked_amp, row, precision=lax.Precision.HIGHEST,
                          preferred_element_type=jnp.float32)

    ladder = jnp.transpose(lax.map(one_row, masked_int), (1, 2, 0, 3))
    anti = ladder - jnp.transpose(ladder, (1, 0, 2, 3))
    anti = anti - jnp.transpose(anti, (0, 1, 3, 2))
    denom = (occ_energy[:, None, None, None] + occ_energy[None, :, None, None]
             - vir_energy[None, None, :, None] - vir_energy[None, None, None, :])
    return anti / denom
```

```python
import functools

import jax
import jax.numpy as jnp
from jax import lax
from jax.experimental import pallas as pl
from jax.experimental.pallas import tpu as pltpu
from jax.sharding import PartitionSpec as P

MESH = pl.DeviceIdType.MESH
F32 = jnp.float32
BF16 = jnp.bfloat16

LANES = 128
TAIL = 64
CAP = LANES + TAIL
CHUNKS = 2

OWN, XP, XM, X2 = (0, 0, 0), (1, 0, 0), (3, 0, 0), (2, 0, 0)
Z, ZP, ZM, Z2 = (0, 1, 0), (1, 1, 0), (3, 1, 0), (2, 1, 0)
CORE = (0, 0, 1)
STAGES = (
    ((OWN, None, Z), (OWN, None, XP), (OWN, None, XM), (OWN, None, CORE)),
    ((Z, None, XP), (Z, None, XM), (XM, 0, XP), (XP, 1, XM), (Z, None, CORE), (XM, None, CORE), (XP, None, CORE)),
    ((X2, 0, Z), (X2, 1, Z), (X2, 0, CORE), (X2, 1, CORE), (ZM, None, CORE), (ZP, None, CORE)),
    ((Z2, 0, CORE), (Z2, 1, CORE)),
)


def gather_ops():
    ops, arrived = [], {}
    for tick in range(len(STAGES) + CHUNKS - 1):
        for chunk in range(CHUNKS):
            if not 0 <= tick - chunk < len(STAGES):
                continue
            for whose, half, route in STAGES[tick - chunk]:
                there = tuple((k - r) % n for k, r, n in zip(whose, route, (4, 2, 2)))
                after = []
                if whose != OWN:
                    for h in (0, 1, None):
                        if (chunk, whose, h) in arrived and (half is None or h is None or h == half):
                            after.append(arrived[chunk, whose, h])
                arrived[chunk, there, half] = len(ops)
                ops.append((chunk, whose, half, route, tuple(after)))
    return ops


GATHER = gather_ops()


def split(x):
    high = x.astype(BF16)
    return high, (x - high.astype(F32)).astype(BF16)


def dot_t(a, b):
    return lax.dot_general(a, b, (((1,), (1,)), ((), ())), preferred_element_type=F32)


def at_lane(row, index):
    lane = lax.broadcasted_iota(jnp.int32, (index.shape[0], row.shape[1]), 1)
    return jnp.sum(jnp.where(lane == index, row, 0.0), axis=1, keepdims=True)


def iota_col(n):
    return lax.broadcasted_iota(jnp.int32, (n, 1), 0)


def kernel(
    t_hbm, v_hbm, eo_ref, ev_ref, so_ref, sv_ref, pair_ref, out_ref, over_ref,
    t_buf, v_buf, vm, vt, tm, tt, t_send, t_recv, a_send, a_recv, blocks, weight, a_main, a_tail,
    in_sem, ts_sem, tr_sem, as_sem, ar_sem, gs_sem, gr_sem,
):
    occ, vir = lax.axis_index("occ"), lax.axis_index("vir")
    x, zl, core = occ // 4, (occ // 2) % 2, occ % 2

    def member(step):
        return ((x + step[0]) % 4) * 4 + ((zl + step[1]) % 2) * 2 + (core + step[2]) % 2

    load_v = pltpu.make_async_copy(v_hbm, v_buf, in_sem.at[0])
    load_t = pltpu.make_async_copy(t_hbm, t_buf, in_sem.at[1])
    load_v.start()
    load_t.start()

    others = [(i // 4, (i // 2) % 2, i % 2) for i in range(1, 16)]
    mirror_occ = vir // 2
    mirror_self = mirror_occ == occ
    bar = pltpu.get_barrier_semaphore()
    for step in others:
        pl.semaphore_signal(bar, inc=1, device_id={"occ": member(step)}, device_id_type=MESH)
    for h in range(2):

        @pl.when(jnp.logical_not(jnp.logical_and(mirror_self, vir % 2 == h)))
        def _():
            pl.semaphore_signal(bar, inc=1, device_id={"occ": mirror_occ, "vir": 2 * occ + h}, device_id_type=MESH)

    pair = pair_ref[...]
    hot = jnp.where(pair == lax.broadcasted_iota(jnp.int32, (8, pair.shape[1]), 0), 1.0, 0.0)
    upper = lax.broadcasted_iota(jnp.int32, (128, 128), 0) <= lax.broadcasted_iota(jnp.int32, (128, 128), 1)
    upper = jnp.where(upper, 1.0, 0.0).astype(BF16)
    parts = [hot[:, 128 * c : 128 * (c + 1)] for c in range(8)]
    counted = jnp.dot(jnp.concatenate(parts, axis=0).astype(BF16), upper, preferred_element_type=F32)
    before = jnp.zeros((8, 1), F32)
    ranks = []
    for c in range(8):
        here = counted[8 * c : 8 * (c + 1)]
        ranks.append(jnp.sum(parts[c] * (here + before), axis=0, keepdims=True))
        before = before + here[:, 127:128]
    rank = jnp.concatenate(ranks, axis=1) - 1.0
    over_ref[...] = jnp.broadcast_to(jnp.max(before, axis=0, keepdims=True), over_ref.shape).astype(jnp.int32)
    lane_of = iota_col(2 * LANES)
    lane_of = jnp.where(lane_of < CAP, lane_of, lane_of - TAIL).astype(F32)
    place = jnp.where(rank == lane_of, 1.0, 0.0).astype(BF16)

    sv_row = sv_ref[...].astype(F32)
    so_row = so_ref[...].astype(F32)
    first_half = lax.broadcasted_iota(jnp.int32, (1, LANES), 1) < TAIL

    def compact(values, sym):
        high, low = split(jnp.where(pair == sym, values, 0.0))
        return dot_t(high, place) + dot_t(low, place)

    rows = iota_col(128)
    sym_v = at_lane(sv_row, 8 * vir + rows // 16).astype(jnp.int32) ^ at_lane(sv_row, 16 * occ + rows % 16).astype(jnp.int32)
    load_v.wait()
    small = compact(v_buf[...].reshape(128, 1024), sym_v)
    vm[...] = small[:, :LANES]
    vt[...] = small[:, LANES:]
    for h in range(2):
        for q in range(4):
            for t in range(2):
                t_send[h, 3 * q + t] = vm[pl.ds(8 * h + q + 4 * t, 8, stride=16), :]
            t_send[h, 3 * q + 2] = jnp.where(
                first_half, vt[pl.ds(8 * h + q, 8, stride=16), :], vt[pl.ds(8 * h + q + 4, 8, stride=16), :]
            )

    @pl.when(mirror_self)
    def _():
        pl.semaphore_wait(bar, 16)

    @pl.when(jnp.logical_not(mirror_self))
    def _():
        pl.semaphore_wait(bar, 17)

    def mirror(h, slot):
        return pltpu.make_async_remote_copy(
            src_ref=t_send.at[h],
            dst_ref=t_recv.at[slot],
            send_sem=ts_sem.at[h],
            recv_sem=tr_sem.at[slot],
            device_id={"occ": mirror_occ, "vir": 2 * occ + h},
            device_id_type=MESH,
        )

    for h in range(2):
        to_self = jnp.logical_and(mirror_self, vir % 2 == h)

        @pl.when(to_self)
        def _():
            t_recv[h] = t_send[h]

        @pl.when(jnp.logical_not(to_self))
        def _():
            mirror(h, vir % 2).start()

    rows = iota_col(256)
    sym_t = at_lane(so_row, 4 * occ + rows // 64).astype(jnp.int32) ^ at_lane(so_row, rows % 64).astype(jnp.int32)
    load_t.wait()
    small = compact(t_buf[...].reshape(256, 1024), sym_t)
    tm[...] = small[:, :LANES]
    tt[...] = small[:, LANES:]
    for i in range(4):
        for j in range(4):
            a_send[pl.ds(4 * i + j, 16, stride=24), :] = tm[pl.ds(64 * i + j, 16, stride=4), :]
        for j in range(2):
            a_send[pl.ds(16 + 2 * i + j, 16, stride=24), :] = jnp.where(
                first_half, tt[pl.ds(64 * i + j, 16, stride=4), :], tt[pl.ds(64 * i + j + 2, 16, stride=4), :]
            )

    def swap(n, step):
        there = member(step)
        return pltpu.make_async_remote_copy(
            src_ref=a_send.at[pl.ds(pl.multiple_of(24 * there, 8), 24), :],
            dst_ref=a_recv.at[pl.ds(pl.multiple_of(24 * occ, 8), 24), :],
            send_sem=as_sem.at[n],
            recv_sem=ar_sem.at[n],
            device_id={"occ": there},
            device_id_type=MESH,
        )

    swaps = [swap(n, step) for n, step in enumerate(others)]
    for copy in swaps:
        copy.start()
    mine = pl.ds(pl.multiple_of(24 * occ, 8), 24)
    a_recv[mine, :] = a_send[mine, :]

    j_of = 4 * (rows % 16) + (rows // 16) % 4
    sym_ij = at_lane(so_row, 4 * occ + rows // 64).astype(jnp.int32) ^ at_lane(so_row, j_of).astype(jnp.int32)
    eo_row, ev_row = eo_ref[...], ev_ref[...]
    e_ij = at_lane(eo_row, 4 * occ + rows // 64) + at_lane(eo_row, j_of)
    sv_int = sv_ref[...]

    def weigh(a, carry):
        which = jnp.full((1, 1), 8 * vir + a, jnp.int32)
        sym_b = sv_int ^ at_lane(sv_row, which).astype(jnp.int32)
        e_b = at_lane(ev_row, which) + ev_row
        weight[a] = jnp.where(sym_ij == sym_b, 1.0 / (e_ij - e_b), 0.0)
        return carry

    lax.fori_loop(0, 8, weigh, 0)

    here = pl.multiple_of(16 * occ, 16)
    for g in range(2):
        from_self = jnp.logical_and(mirror_self, vir % 2 == g)

        @pl.when(jnp.logical_not(from_self))
        def _():
            mirror(g, g).wait_recv()

        for q in range(4):
            for t in range(2):
                own = vm[pl.ds(16 * (q + 4 * t) + 8 * g, 8), :]
                blocks[3 * q + t, pl.ds(here + 8 * g, 8), :] = own - t_recv[g, 3 * q + t]
            own = jnp.where(first_half, vt[pl.ds(16 * q + 8 * g, 8), :], vt[pl.ds(16 * (q + 4) + 8 * g, 8), :])
            blocks[3 * q + 2, pl.ds(here + 8 * g, 8), :] = own - t_recv[g, 3 * q + 2]

    width = 12 // CHUNKS

    def hop(n):
        chunk, whose, half, route, _ = GATHER[n]
        first = 16 * member(whose)
        size = 16
        if half is not None:
            first, size = first + 8 * half, 8
        part = blocks.at[pl.ds(chunk * width, width), pl.ds(pl.multiple_of(first, 8), size), :]
        return pltpu.make_async_remote_copy(
            src_ref=part,
            dst_ref=part,
            send_sem=gs_sem.at[n],
            recv_sem=gr_sem.at[n],
            device_id={"occ": member(route)},
            device_id_type=MESH,
        )

    def landing(n):
        chunk, whose, half, route, _ = GATHER[n]
        back = tuple((k - r) % m for k, r, m in zip(whose, route, (4, 2, 2)))
        first = 16 * member(back)
        size = 16
        if half is not None:
            first, size = first + 8 * half, 8
        part = blocks.at[pl.ds(chunk * width, width), pl.ds(pl.multiple_of(first, 8), size), :]
        return pltpu.make_async_remote_copy(
            src_ref=part,
            dst_ref=part,
            send_sem=gs_sem.at[n],
            recv_sem=gr_sem.at[n],
            device_id={"occ": member(route)},
            device_id_type=MESH,
        )

    arrived = set()

    def need(n):
        if n not in arrived:
            arrived.add(n)
            landing(n).wait_recv()

    def antisymmetrize_amplitudes():
        for n, copy in enumerate(swaps):
            copy.wait_recv()
        for i in range(4):
            for j in range(4):
                to = pl.ds(64 * i + 16 * j, 16)
                a_main[to, :] = tm[pl.ds(64 * i + j, 16, stride=4), :] - a_recv[pl.ds(4 * j + i, 16, stride=24), :]
                tail = a_recv[pl.ds(16 + 2 * j + i % 2, 16, stride=24), :]
                turned = pltpu.roll(tail, TAIL, 1)
                tail = jnp.where(first_half, tail, turned) if i < 2 else jnp.where(first_half, turned, tail)
                a_tail[to, :] = tt[pl.ds(64 * i + j, 16, stride=4), :] - tail

    prepared = []

    def multiply(chunk):
        if not prepared:
            antisymmetrize_amplitudes()
            main = a_main[...]
            tail = a_tail[...]
            for t in range(2):
                kept = jnp.where(first_half if t == 0 else jnp.logical_not(first_half), tail, 0.0)
                prepared.append(split(jnp.concatenate([main, kept], axis=1)))
        for q in range(chunk * width // 3, (chunk + 1) * width // 3):
            for t in range(2):
                a_high, a_low = prepared[t]
                b_high, b_low = split(jnp.concatenate([blocks[3 * q + t], blocks[3 * q + 2]], axis=1))
                c = dot_t(a_high, b_high) + (dot_t(a_low, b_high) + dot_t(a_high, b_low))
                c = c * weight[q + 4 * t]
                for i in range(4):
                    for j in range(4):
                        part = c[64 * i + 16 * j : 64 * i + 16 * (j + 1)]
                        for s in range(2):
                            out_ref[s, pl.ds(8 * (64 * i + j) + q + 4 * t, 16, stride=32), :] = part[
                                :, 128 * s : 128 * (s + 1)
                            ]

    for n, op in enumerate(GATHER):
        for m in op[4]:
            need(m)
        hop(n).start()
    for chunk in range(CHUNKS):
        for n, op in enumerate(GATHER):
            if op[0] == chunk:
                need(n)
        multiply(chunk)

    for h in range(2):

        @pl.when(jnp.logical_not(jnp.logical_and(mirror_self, vir % 2 == h)))
        def _():
            mirror(h, vir % 2).wait_send()

    for copy in swaps:
        copy.wait_send()
    for n in range(len(GATHER)):
        hop(n).wait_send()


def compacted(amplitudes, integrals, occ_energy, vir_energy, occ_irrep, vir_irrep, pair_irrep):
    whole = pl.BlockSpec(memory_space=pltpu.VMEM)
    away = pl.BlockSpec(memory_space=pl.ANY)
    sems = pltpu.SemaphoreType.DMA
    out, over = pl.pallas_call(
        kernel,
        out_shape=(
            jax.ShapeDtypeStruct((2, 2048, 128), F32),
            jax.ShapeDtypeStruct((8, 128), jnp.int32),
        ),
        in_specs=[away, away] + [whole] * 5,
        out_specs=(whole, whole),
        scratch_shapes=[
            pltpu.VMEM((4, 64, 1024), F32),
            pltpu.VMEM((8, 16, 1024), F32),
            pltpu.VMEM((128, LANES), F32),
            pltpu.VMEM((128, LANES), F32),
            pltpu.VMEM((256, LANES), F32),
            pltpu.VMEM((256, LANES), F32),
            pltpu.VMEM((2, 12, 8, LANES), F32),
            pltpu.VMEM((2, 12, 8, LANES), F32),
            pltpu.VMEM((16 * 24, LANES), F32),
            pltpu.VMEM((16 * 24, LANES), F32),
            pltpu.VMEM((12, 256, LANES), F32),
            pltpu.VMEM((8, 256, 256), F32),
            pltpu.VMEM((256, LANES), F32),
            pltpu.VMEM((256, LANES), F32),
            sems((2,)),
            sems((2,)),
            sems((2,)),
            sems((15,)),
            sems((15,)),
            sems((len(GATHER),)),
            sems((len(GATHER),)),
        ],
        compiler_params=pltpu.CompilerParams(collective_id=0, has_side_effects=True, vmem_limit_bytes=40 * 2**20),
        name="ladder",
    )(
        amplitudes,
        integrals,
        occ_energy.reshape(1, -1),
        vir_energy.reshape(1, -1),
        occ_irrep.reshape(1, -1),
        vir_irrep.reshape(1, -1),
        pair_irrep.reshape(1, -1),
    )
    out = jnp.transpose(out.reshape(2, 4, 64, 8, 128), (1, 2, 3, 0, 4)).reshape(4, 64, 8, 256)
    return out, over[0, 0]


def dense(amplitudes, integrals, occ_energy, vir_energy, occ_irrep, vir_irrep, pair_irrep):
    occ_rows = amplitudes.shape[0]
    vir_rows = integrals.shape[0]
    vir_cols = integrals.shape[1]
    occ_start = lax.axis_index("occ") * occ_rows
    vir_start = lax.axis_index("vir") * vir_rows
    col_start = lax.axis_index("occ") * vir_cols
    own_occ = lax.dynamic_slice_in_dim(occ_irrep, occ_start, occ_rows)
    pair_sym = jnp.bitwise_xor(own_occ[:, None], occ_irrep[None, :])
    masked_amp = jnp.where(
        pair_sym[:, :, None] == pair_irrep[None, None, :], amplitudes, jnp.float32(0.0)
    )
    own_vir = lax.dynamic_slice_in_dim(vir_irrep, vir_start, vir_rows)
    col_vir = lax.dynamic_slice_in_dim(vir_irrep, col_start, vir_cols)
    vir_sym = jnp.bitwise_xor(own_vir[:, None], col_vir[None, :])
    masked_int = jnp.where(
        vir_sym[:, :, None] == pair_irrep[None, None, :], integrals, jnp.float32(0.0)
    )
    ladder = jnp.einsum(
        "ijk,abk->ijab",
        masked_amp,
        lax.all_gather(masked_int, "occ", axis=1, tiled=True),
        precision=lax.Precision.HIGHEST,
        preferred_element_type=jnp.float32,
    )
    ladder_swap = lax.all_to_all(ladder, "occ", split_axis=1, concat_axis=0, tiled=True)
    occ_anti = ladder - jnp.transpose(ladder_swap, (1, 0, 2, 3))
    virt_swap = lax.all_to_all(occ_anti, "vir", split_axis=3, concat_axis=2, tiled=True)
    anti = occ_anti - jnp.transpose(virt_swap, (0, 1, 3, 2))
    own_occ_energy = lax.dynamic_slice_in_dim(occ_energy, occ_start, occ_rows)
    own_vir_energy = lax.dynamic_slice_in_dim(vir_energy, vir_start, vir_rows)
    denom = (
        own_occ_energy[:, None, None, None]
        + occ_energy[None, :, None, None]
        - own_vir_energy[None, None, :, None]
        - vir_energy[None, None, None, :]
    )
    return anti / denom


def local(*args):
    out, most = compacted(*args)
    return lax.cond(most > CAP, lambda out: dense(*args), lambda out: out, out)


def solution(mesh):
    placed = (P("occ", None, None), P("vir", "occ", None), P(), P(), P(), P(), P())
    return jax.shard_map(
        local, mesh=mesh, in_specs=placed, out_specs=P("occ", None, "vir", None), check_vma=False
    )
```

```python
import functools

import jax
import jax.numpy as jnp
from jax import lax
from jax.experimental import pallas as pl
from jax.experimental.pallas import tpu as pltpu
from jax.sharding import PartitionSpec as P

MESH = pl.DeviceIdType.MESH
F32 = jnp.float32
BF16 = jnp.bfloat16

LANES = 128
TAIL = 64
CAP = LANES + TAIL
CHUNKS = 2

OWN, CORE = (0, 0, 0), (0, 0, 1)
SAME = ((2, 1, 0), (2, 0, 0), (1, 1, 0), (3, 1, 0), (1, 0, 0), (3, 0, 0), (0, 1, 0))
STAGES = (
    tuple((OWN, step) for step in SAME) + ((OWN, CORE),),
    tuple((((-step[0]) % 4, step[1], 0), CORE) for step in reversed(SAME)),
)


def gather_ops():
    ops, arrived = [], {}
    for tick in range(len(STAGES) + CHUNKS - 1):
        for chunk in range(CHUNKS):
            if not 0 <= tick - chunk < len(STAGES):
                continue
            for whose, route in STAGES[tick - chunk]:
                there = tuple((k - r) % n for k, r, n in zip(whose, route, (4, 2, 2)))
                after = arrived[chunk, whose] if whose != OWN else None
                arrived[chunk, there] = len(ops)
                ops.append((chunk, whose, route, after))
    return ops


GATHER = gather_ops()


def split(x):
    high = x.astype(BF16)
    return high, (x - high.astype(F32)).astype(BF16)


def dot_t(a, b):
    return lax.dot_general(a, b, (((1,), (1,)), ((), ())), preferred_element_type=F32)


def at_lane(row, index):
    lane = lax.broadcasted_iota(jnp.int32, (index.shape[0], row.shape[1]), 1)
    return jnp.sum(jnp.where(lane == index, row, 0.0), axis=1, keepdims=True)


def iota_col(n):
    return lax.broadcasted_iota(jnp.int32, (n, 1), 0)


def kernel(
    t_hbm, v_hbm, eo_ref, ev_ref, so_ref, sv_ref, pair_ref, turn_ref, out_ref, most_ref,
    t_buf, v_buf, vm, vt, tm, tt, t_send, t_recv, a_send, a_recv, blocks, weight, a_main, a_tail,
    in_sem, ts_sem, tr_sem, as_sem, ar_sem, gs_sem, gr_sem,
):
    occ, vir = lax.axis_index("occ"), lax.axis_index("vir")
    x, zl, core = occ // 4, (occ // 2) % 2, occ % 2

    def member(step):
        return ((x + step[0]) % 4) * 4 + ((zl + step[1]) % 2) * 2 + (core + step[2]) % 2

    load_v = pltpu.make_async_copy(v_hbm, v_buf, in_sem.at[0])
    load_t = pltpu.make_async_copy(t_hbm, t_buf, in_sem.at[1])
    load_v.start()
    load_t.start()

    others = [(i // 4, (i // 2) % 2, i % 2) for i in range(1, 16)]
    mirror_occ = vir // 2
    mirror_self = mirror_occ == occ
    bar = pltpu.get_barrier_semaphore()
    for step in others:
        pl.semaphore_signal(bar, inc=1, device_id={"occ": member(step)}, device_id_type=MESH)
    for h in range(2):

        @pl.when(jnp.logical_not(jnp.logical_and(mirror_self, vir % 2 == h)))
        def _():
            pl.semaphore_signal(bar, inc=1, device_id={"occ": mirror_occ, "vir": 2 * occ + h}, device_id_type=MESH)

    pair = pair_ref[...]
    hot = jnp.where(pair == lax.broadcasted_iota(jnp.int32, (8, pair.shape[1]), 0), 1.0, 0.0)
    upper = lax.broadcasted_iota(jnp.int32, (128, 128), 0) <= lax.broadcasted_iota(jnp.int32, (128, 128), 1)
    upper = jnp.where(upper, 1.0, 0.0).astype(BF16)
    parts = [hot[:, 128 * c : 128 * (c + 1)] for c in range(8)]
    counted = jnp.dot(jnp.concatenate(parts, axis=0).astype(BF16), upper, preferred_element_type=F32)
    before = jnp.zeros((8, 1), F32)
    ranks = []
    for c in range(8):
        here = counted[8 * c : 8 * (c + 1)]
        ranks.append(jnp.sum(parts[c] * (here + before), axis=0, keepdims=True))
        before = before + here[:, 127:128]
    rank = jnp.concatenate(ranks, axis=1) - 1.0 - CAP * turn_ref[...].astype(F32)
    most_ref[...] = jnp.broadcast_to(jnp.max(before, axis=0, keepdims=True), most_ref.shape).astype(jnp.int32)
    lane_of = iota_col(2 * LANES)
    lane_of = jnp.where(lane_of < CAP, lane_of, lane_of - TAIL).astype(F32)
    place = jnp.where(rank == lane_of, 1.0, 0.0).astype(BF16)

    sv_row = sv_ref[...].astype(F32)
    so_row = so_ref[...].astype(F32)
    first_half = lax.broadcasted_iota(jnp.int32, (1, LANES), 1) < TAIL

    def compact(values, sym):
        high, low = split(jnp.where(pair == sym, values, 0.0))
        return dot_t(high, place) + dot_t(low, place)

    rows = iota_col(128)
    sym_v = at_lane(sv_row, 8 * vir + rows // 16).astype(jnp.int32) ^ at_lane(sv_row, 16 * occ + rows % 16).astype(jnp.int32)
    load_v.wait()
    small = compact(v_buf[...].reshape(128, 1024), sym_v)
    vm[...] = small[:, :LANES]
    vt[...] = small[:, LANES:]
    for h in range(2):
        for q in range(4):
            for t in range(2):
                t_send[h, 3 * q + t] = vm[pl.ds(8 * h + q + 4 * t, 8, stride=16), :]
            t_send[h, 3 * q + 2] = jnp.where(
                first_half, vt[pl.ds(8 * h + q, 8, stride=16), :], vt[pl.ds(8 * h + q + 4, 8, stride=16), :]
            )

    @pl.when(mirror_self)
    def _():
        pl.semaphore_wait(bar, 16)

    @pl.when(jnp.logical_not(mirror_self))
    def _():
        pl.semaphore_wait(bar, 17)

    def mirror(h, slot):
        return pltpu.make_async_remote_copy(
            src_ref=t_send.at[h],
            dst_ref=t_recv.at[slot],
            send_sem=ts_sem.at[h],
            recv_sem=tr_sem.at[slot],
            device_id={"occ": mirror_occ, "vir": 2 * occ + h},
            device_id_type=MESH,
        )

    for h in range(2):
        to_self = jnp.logical_and(mirror_self, vir % 2 == h)

        @pl.when(to_self)
        def _():
            t_recv[h] = t_send[h]

        @pl.when(jnp.logical_not(to_self))
        def _():
            mirror(h, vir % 2).start()

    rows = iota_col(256)
    sym_t = at_lane(so_row, 4 * occ + rows // 64).astype(jnp.int32) ^ at_lane(so_row, rows % 64).astype(jnp.int32)
    load_t.wait()
    small = compact(t_buf[...].reshape(256, 1024), sym_t)
    tm[...] = small[:, :LANES]
    tt[...] = small[:, LANES:]
    for i in range(4):
        for j in range(4):
            a_send[pl.ds(4 * i + j, 16, stride=24), :] = tm[pl.ds(64 * i + j, 16, stride=4), :]
        for j in range(2):
            a_send[pl.ds(16 + 2 * i + j, 16, stride=24), :] = jnp.where(
                first_half, tt[pl.ds(64 * i + j, 16, stride=4), :], tt[pl.ds(64 * i + j + 2, 16, stride=4), :]
            )

    def swap(n, step):
        there = member(step)
        return pltpu.make_async_remote_copy(
            src_ref=a_send.at[pl.ds(pl.multiple_of(24 * there, 8), 24), :],
            dst_ref=a_recv.at[pl.ds(pl.multiple_of(24 * occ, 8), 24), :],
            send_sem=as_sem.at[n],
            recv_sem=ar_sem.at[n],
            device_id={"occ": there},
            device_id_type=MESH,
        )

    swaps = [swap(n, step) for n, step in enumerate(others)]
    for copy in swaps:
        copy.start()
    mine = pl.ds(pl.multiple_of(24 * occ, 8), 24)
    a_recv[mine, :] = a_send[mine, :]

    eo_row, ev_row = eo_ref[...], ev_ref[...]
    e_ij = at_lane(eo_row, 4 * occ + rows // 64) + at_lane(eo_row, rows % 64)
    sv_int = sv_ref[...]

    def weigh(a, carry):
        which = jnp.full((1, 1), 8 * vir + a, jnp.int32)
        sym_b = sv_int ^ at_lane(sv_row, which).astype(jnp.int32)
        e_b = at_lane(ev_row, which) + ev_row
        weight[a] = jnp.where(sym_t == sym_b, 1.0 / (e_ij - e_b), 0.0)
        return carry

    lax.fori_loop(0, 8, weigh, 0)

    here = pl.multiple_of(16 * occ, 16)
    for g in range(2):
        from_self = jnp.logical_and(mirror_self, vir % 2 == g)

        @pl.when(jnp.logical_not(from_self))
        def _():
            mirror(g, g).wait_recv()

        for q in range(4):
            for t in range(2):
                own = vm[pl.ds(16 * (q + 4 * t) + 8 * g, 8), :]
                blocks[3 * q + t, pl.ds(here + 8 * g, 8), :] = own - t_recv[g, 3 * q + t]
            own = jnp.where(first_half, vt[pl.ds(16 * q + 8 * g, 8), :], vt[pl.ds(16 * (q + 4) + 8 * g, 8), :])
            blocks[3 * q + 2, pl.ds(here + 8 * g, 8), :] = own - t_recv[g, 3 * q + 2]

    width = 12 // CHUNKS

    def hop(n, landing=False):
        chunk, whose, route, _ = GATHER[n]
        if landing:
            whose = tuple((k - r) % m for k, r, m in zip(whose, route, (4, 2, 2)))
        part = blocks.at[pl.ds(chunk * width, width), pl.ds(pl.multiple_of(16 * member(whose), 16), 16), :]
        return pltpu.make_async_remote_copy(
            src_ref=part,
            dst_ref=part,
            send_sem=gs_sem.at[n],
            recv_sem=gr_sem.at[n],
            device_id={"occ": member(route)},
            device_id_type=MESH,
        )

    arrived = set()

    def need(n):
        if n not in arrived:
            arrived.add(n)
            hop(n, landing=True).wait_recv()

    def antisymmetrize_amplitudes():
        for n, copy in enumerate(swaps):
            copy.wait_recv()
        for i in range(4):
            for j in range(4):
                to = pl.ds(64 * i + j, 16, stride=4)
                a_main[to, :] = tm[to, :] - a_recv[pl.ds(4 * j + i, 16, stride=24), :]
                tail = a_recv[pl.ds(16 + 2 * j + i % 2, 16, stride=24), :]
                turned = pltpu.roll(tail, TAIL, 1)
                tail = jnp.where(first_half, tail, turned) if i < 2 else jnp.where(first_half, turned, tail)
                a_tail[to, :] = tt[to, :] - tail

    prepared = []

    def multiply(chunk):
        if not prepared:
            antisymmetrize_amplitudes()
            main = a_main[...]
            tail = a_tail[...]
            for t in range(2):
                kept = jnp.where(first_half if t == 0 else jnp.logical_not(first_half), tail, 0.0)
                prepared.append(split(jnp.concatenate([main, kept], axis=1)))
        for q in range(chunk * width // 3, (chunk + 1) * width // 3):
            for t in range(2):
                a_high, a_low = prepared[t]
                b_high, b_low = split(jnp.concatenate([blocks[3 * q + t], blocks[3 * q + 2]], axis=1))
                c = dot_t(a_high, b_high) + (dot_t(a_low, b_high) + dot_t(a_high, b_low))
                out_ref[q + 4 * t] = c * weight[q + 4 * t]

    for n, op in enumerate(GATHER):
        if op[3] is not None:
            need(op[3])
        hop(n).start()
    for chunk in range(CHUNKS):
        for n, op in enumerate(GATHER):
            if op[0] == chunk:
                need(n)
        multiply(chunk)

    for h in range(2):

        @pl.when(jnp.logical_not(jnp.logical_and(mirror_self, vir % 2 == h)))
        def _():
            mirror(h, vir % 2).wait_send()

    for copy in swaps:
        copy.wait_send()
    for n in range(len(GATHER)):
        hop(n).wait_send()


def one_pass(turn, amplitudes, integrals, occ_energy, vir_energy, occ_irrep, vir_irrep, pair_irrep):
    whole = pl.BlockSpec(memory_space=pltpu.VMEM)
    away = pl.BlockSpec(memory_space=pl.ANY)
    sems = pltpu.SemaphoreType.DMA
    out, most = pl.pallas_call(
        kernel,
        out_shape=(
            jax.ShapeDtypeStruct((8, 256, 256), F32),
            jax.ShapeDtypeStruct((1, 1), jnp.int32),
        ),
        in_specs=[away, away] + [whole] * 6,
        out_specs=(whole, whole),
        scratch_shapes=[
            pltpu.VMEM((4, 64, 1024), F32),
            pltpu.VMEM((8, 16, 1024), F32),
            pltpu.VMEM((128, LANES), F32),
            pltpu.VMEM((128, LANES), F32),
            pltpu.VMEM((256, LANES), F32),
            pltpu.VMEM((256, LANES), F32),
            pltpu.VMEM((2, 12, 8, LANES), F32),
            pltpu.VMEM((2, 12, 8, LANES), F32),
            pltpu.VMEM((16 * 24, LANES), F32),
            pltpu.VMEM((16 * 24, LANES), F32),
            pltpu.VMEM((12, 256, LANES), F32),
            pltpu.VMEM((8, 256, 256), F32),
            pltpu.VMEM((256, LANES), F32),
            pltpu.VMEM((256, LANES), F32),
            sems((2,)),
            sems((2,)),
            sems((2,)),
            sems((15,)),
            sems((15,)),
            sems((len(GATHER),)),
            sems((len(GATHER),)),
        ],
        compiler_params=pltpu.CompilerParams(collective_id=0, has_side_effects=True, vmem_limit_bytes=40 * 2**20),
        name="ladder",
    )(
        amplitudes,
        integrals,
        occ_energy.reshape(1, -1),
        vir_energy.reshape(1, -1),
        occ_irrep.reshape(1, -1),
        vir_irrep.reshape(1, -1),
        pair_irrep.reshape(1, -1),
        turn,
    )
    return out, most


def local(*args):
    turn = jnp.zeros((1, 1), jnp.int32)
    out, most = one_pass(turn, *args)

    def more(state):
        return (CAP * (state[0] + 1) < most)[0, 0]

    def step(state):
        turn = state[0] + 1
        return turn, state[1] + one_pass(turn, *args)[0]

    _, out = lax.while_loop(more, step, (turn, out))
    return jnp.transpose(out.reshape(8, 4, 64, 256), (1, 2, 0, 3))


def solution(mesh):
    placed = (P("occ", None, None), P("vir", "occ", None), P(), P(), P(), P(), P())
    return jax.shard_map(
        local, mesh=mesh, in_specs=placed, out_specs=P("occ", None, "vir", None), check_vma=False
    )
```

```python
import functools

import jax
import jax.numpy as jnp
from jax import lax
from jax.experimental import pallas as pl
from jax.experimental.pallas import tpu as pltpu
from jax.sharding import PartitionSpec as P

MESH = pl.DeviceIdType.MESH
F32 = jnp.float32
BF16 = jnp.bfloat16

LANES = 128
TAIL = 64
CAP = LANES + TAIL

OWN, XP, XM, X2 = (0, 0, 0), (1, 0, 0), (3, 0, 0), (2, 0, 0)
Z, ZP, ZM, Z2 = (0, 1, 0), (1, 1, 0), (3, 1, 0), (2, 1, 0)
CORE = (0, 0, 1)
CHIPS = (Z2, X2, ZP, ZM, XP, XM, Z)
ROUTES = (
    (OWN, X2), (OWN, Z), (OWN, XP), (OWN, XM), (OWN, CORE),
    (Z, XP), (Z, XM), (Z, CORE),
    (X2, Z), (X2, CORE),
    (XP, CORE), (XM, CORE), (ZM, CORE), (ZP, CORE), (Z2, CORE),
)


def gather_ops():
    ops, arrived = [], {}
    for whose, route in ROUTES:
        there = tuple((k - r) % n for k, r, n in zip(whose, route, (4, 2, 2)))
        after = arrived[whose] if whose != OWN else None
        arrived[there] = len(ops)
        ops.append((whose, route, after))
    return ops


GATHER = gather_ops()


def split(x):
    high = x.astype(BF16)
    return high, (x - high.astype(F32)).astype(BF16)


def dot_t(a, b):
    return lax.dot_general(a, b, (((1,), (1,)), ((), ())), preferred_element_type=F32)


def at_lane(row, index):
    lane = lax.broadcasted_iota(jnp.int32, (index.shape[0], row.shape[1]), 1)
    return jnp.sum(jnp.where(lane == index, row, 0.0), axis=1, keepdims=True)


def iota_col(n):
    return lax.broadcasted_iota(jnp.int32, (n, 1), 0)


def kernel(
    t_hbm, v_hbm, eo_hbm, ev_hbm, so_hbm, sv_hbm, pair_hbm, turn_hbm, out_ref, most_ref,
    t_buf, v_buf, eo_ref, ev_ref, so_ref, sv_ref, pair_ref, turn_ref, vm, vt, tm, tt, t_send, t_recv, a_send, a_pair, a_recv,
    blocks, weight, a_main, a_tail, in_sem, ts_sem, tr_sem, as_sem, ar_sem, gs_sem, gr_sem,
):
    occ, vir = lax.axis_index("occ"), lax.axis_index("vir")
    x, zl, core = occ // 4, (occ // 2) % 2, occ % 2

    def member(step):
        return ((x + step[0]) % 4) * 4 + ((zl + step[1]) % 2) * 2 + (core + step[2]) % 2

    mirror_occ = vir // 2
    mirror_self = mirror_occ == occ
    bar = pltpu.get_barrier_semaphore()
    for h in range(2):

        @pl.when(jnp.logical_not(jnp.logical_and(mirror_self, vir % 2 == h)))
        def _():
            pl.semaphore_signal(bar, inc=1, device_id={"occ": mirror_occ, "vir": 2 * occ + h}, device_id_type=MESH)

    for step in CHIPS + (CORE,):
        pl.semaphore_signal(bar, inc=1, device_id={"occ": member(step)}, device_id_type=MESH)

    loads = [
        pltpu.make_async_copy(src, dst, in_sem.at[n])
        for n, (src, dst) in enumerate(
            (
                (pair_hbm, pair_ref), (turn_hbm, turn_ref), (sv_hbm, sv_ref), (v_hbm, v_buf),
                (so_hbm, so_ref), (t_hbm, t_buf), (eo_hbm, eo_ref), (ev_hbm, ev_ref),
            )
        )
    ]
    for load in loads:
        load.start()
    loads[0].wait()
    loads[1].wait()

    pair = pair_ref[...]
    hot = jnp.where(pair == lax.broadcasted_iota(jnp.int32, (8, pair.shape[1]), 0), 1.0, 0.0)
    upper = lax.broadcasted_iota(jnp.int32, (128, 128), 0) <= lax.broadcasted_iota(jnp.int32, (128, 128), 1)
    upper = jnp.where(upper, 1.0, 0.0).astype(BF16)
    parts = [hot[:, 128 * c : 128 * (c + 1)] for c in range(8)]
    counted = jnp.dot(jnp.concatenate(parts, axis=0).astype(BF16), upper, preferred_element_type=F32)
    before = jnp.zeros((8, 1), F32)
    ranks = []
    for c in range(8):
        here = counted[8 * c : 8 * (c + 1)]
        ranks.append(jnp.sum(parts[c] * (here + before), axis=0, keepdims=True))
        before = before + here[:, 127:128]
    rank = jnp.concatenate(ranks, axis=1) - 1.0 - CAP * turn_ref[...].astype(F32)
    most_ref[...] = jnp.broadcast_to(jnp.max(before, axis=0, keepdims=True), most_ref.shape).astype(jnp.int32)
    lane_of = iota_col(2 * LANES)
    lane_of = jnp.where(lane_of < CAP, lane_of, lane_of - TAIL).astype(F32)
    place = jnp.where(rank == lane_of, 1.0, 0.0).astype(BF16)

    first_half = lax.broadcasted_iota(jnp.int32, (1, LANES), 1) < TAIL

    def compact(values, sym):
        high, low = split(jnp.where(pair == sym, values, 0.0))
        return dot_t(high, place) + dot_t(low, place)

    loads[2].wait()
    sv_row = sv_ref[...].astype(F32)
    rows = iota_col(128)
    sym_v = at_lane(sv_row, 8 * vir + rows // 16).astype(jnp.int32) ^ at_lane(sv_row, 16 * occ + rows % 16).astype(jnp.int32)
    loads[3].wait()
    small = compact(v_buf[...].reshape(128, 1024), sym_v)
    vm[...] = small[:, :LANES]
    vt[...] = small[:, LANES:]
    for h in range(2):
        for q in range(4):
            for t in range(2):
                t_send[h, 3 * q + t] = vm[pl.ds(8 * h + q + 4 * t, 8, stride=16), :]
            t_send[h, 3 * q + 2] = jnp.where(
                first_half, vt[pl.ds(8 * h + q, 8, stride=16), :], vt[pl.ds(8 * h + q + 4, 8, stride=16), :]
            )

    @pl.when(mirror_self)
    def _():
        pl.semaphore_wait(bar, 9)

    @pl.when(jnp.logical_not(mirror_self))
    def _():
        pl.semaphore_wait(bar, 10)

    def mirror(h, slot):
        return pltpu.make_async_remote_copy(
            src_ref=t_send.at[h],
            dst_ref=t_recv.at[slot],
            send_sem=ts_sem.at[h],
            recv_sem=tr_sem.at[slot],
            device_id={"occ": mirror_occ, "vir": 2 * occ + h},
            device_id_type=MESH,
        )

    for h in range(2):
        to_self = jnp.logical_and(mirror_self, vir % 2 == h)

        @pl.when(to_self)
        def _():
            t_recv[h] = t_send[h]

        @pl.when(jnp.logical_not(to_self))
        def _():
            mirror(h, vir % 2).start()

    loads[4].wait()
    so_row = so_ref[...].astype(F32)
    rows = iota_col(256)
    sym_t = at_lane(so_row, 4 * occ + rows // 64).astype(jnp.int32) ^ at_lane(so_row, rows % 64).astype(jnp.int32)
    loads[5].wait()
    small = compact(t_buf[...].reshape(256, 1024), sym_t)
    tm[...] = small[:, :LANES]
    tt[...] = small[:, LANES:]
    packed = a_send.reshape(2 * 8 * 24, LANES)
    for i in range(4):
        for j in range(4):
            for c in range(2):
                packed[pl.ds(192 * c + 4 * i + j, 8, stride=24), :] = tm[pl.ds(64 * i + 4 * c + j, 8, stride=8), :]
        for j in range(2):
            for c in range(2):
                packed[pl.ds(192 * c + 16 + 2 * i + j, 8, stride=24), :] = jnp.where(
                    first_half,
                    tt[pl.ds(64 * i + 4 * c + j, 8, stride=8), :],
                    tt[pl.ds(64 * i + 4 * c + j + 2, 8, stride=8), :],
                )

    chip = occ // 2
    share = pltpu.make_async_remote_copy(
        src_ref=a_send.at[1 - core],
        dst_ref=a_pair.at[:, core],
        send_sem=as_sem.at[7],
        recv_sem=ar_sem.at[7],
        device_id={"occ": member(CORE)},
        device_id_type=MESH,
    )
    share.start()
    a_pair[:, core] = a_send[core]

    def swap(n, step):
        return pltpu.make_async_remote_copy(
            src_ref=a_pair.at[member(step) // 2],
            dst_ref=a_recv.at[chip],
            send_sem=as_sem.at[n],
            recv_sem=ar_sem.at[n],
            device_id={"occ": member(step)},
            device_id_type=MESH,
        )

    loads[6].wait()
    loads[7].wait()
    eo_row, ev_row = eo_ref[...], ev_ref[...]
    e_ij = at_lane(eo_row, 4 * occ + rows // 64) + at_lane(eo_row, rows % 64)
    sv_int = sv_ref[...]

    def weigh(a, carry):
        which = jnp.full((1, 1), 8 * vir + a, jnp.int32)
        sym_b = sv_int ^ at_lane(sv_row, which).astype(jnp.int32)
        e_b = at_lane(ev_row, which) + ev_row
        weight[a] = jnp.where(sym_t == sym_b, 1.0 / (e_ij - e_b), 0.0)
        return carry

    lax.fori_loop(0, 4, weigh, 0)
    share.wait_recv()
    swaps = [swap(n, step) for n, step in enumerate(CHIPS)]
    for copy in swaps:
        copy.start()
    a_recv[chip] = a_pair[chip]
    lax.fori_loop(4, 8, weigh, 0)

    here = pl.multiple_of(16 * occ, 16)
    for g in range(2):
        from_self = jnp.logical_and(mirror_self, vir % 2 == g)

        @pl.when(jnp.logical_not(from_self))
        def _():
            mirror(g, g).wait_recv()

        for q in range(4):
            for t in range(2):
                own = vm[pl.ds(16 * (q + 4 * t) + 8 * g, 8), :]
                blocks[3 * q + t, pl.ds(here + 8 * g, 8), :] = own - t_recv[g, 3 * q + t]
            own = jnp.where(first_half, vt[pl.ds(16 * q + 8 * g, 8), :], vt[pl.ds(16 * (q + 4) + 8 * g, 8), :])
            blocks[3 * q + 2, pl.ds(here + 8 * g, 8), :] = own - t_recv[g, 3 * q + 2]

    def hop(n, landing=False):
        whose, route, _ = GATHER[n]
        if landing:
            whose = tuple((k - r) % m for k, r, m in zip(whose, route, (4, 2, 2)))
        part = blocks.at[:, pl.ds(pl.multiple_of(16 * member(whose), 16), 16), :]
        return pltpu.make_async_remote_copy(
            src_ref=part,
            dst_ref=part,
            send_sem=gs_sem.at[n],
            recv_sem=gr_sem.at[n],
            device_id={"occ": member(route)},
            device_id_type=MESH,
        )

    arrived = set()

    def need(n):
        if n not in arrived:
            arrived.add(n)
            hop(n, landing=True).wait_recv()

    for n, (_, _, after) in enumerate(GATHER):
        if after is None:
            hop(n).start()

    for copy in swaps:
        copy.wait_recv()
    theirs = a_recv.reshape(16 * 24, LANES)
    for i in range(4):
        for j in range(4):
            to = pl.ds(64 * i + j, 16, stride=4)
            a_main[to, :] = tm[to, :] - theirs[pl.ds(4 * j + i, 16, stride=24), :]
            tail = theirs[pl.ds(16 + 2 * j + i % 2, 16, stride=24), :]
            turned = pltpu.roll(tail, TAIL, 1)
            tail = jnp.where(first_half, tail, turned) if i < 2 else jnp.where(first_half, turned, tail)
            a_tail[to, :] = tt[to, :] - tail
    factors = []
    for t in range(2):
        kept = jnp.where(first_half if t == 0 else jnp.logical_not(first_half), a_tail[...], 0.0)
        high, low = split(jnp.concatenate([a_main[...], kept], axis=1))
        factors.append(jnp.concatenate([high, low, high], axis=1))

    for n, (_, _, after) in enumerate(GATHER):
        if after is not None:
            need(after)
            hop(n).start()
    for n in range(len(GATHER)):
        need(n)

    for q in range(4):
        for t in range(2):
            high, low = split(jnp.concatenate([blocks[3 * q + t], blocks[3 * q + 2]], axis=1))
            c = dot_t(factors[t], jnp.concatenate([high, high, low], axis=1))
            out_ref[q + 4 * t] = c * weight[q + 4 * t]

    for h in range(2):

        @pl.when(jnp.logical_not(jnp.logical_and(mirror_self, vir % 2 == h)))
        def _():
            mirror(h, vir % 2).wait_send()

    share.wait_send()
    for copy in swaps:
        copy.wait_send()
    for n in range(len(GATHER)):
        hop(n).wait_send()


def one_pass(turn, amplitudes, integrals, occ_energy, vir_energy, occ_irrep, vir_irrep, pair_irrep):
    whole = pl.BlockSpec(memory_space=pltpu.VMEM)
    away = pl.BlockSpec(memory_space=pl.ANY)
    sems = pltpu.SemaphoreType.DMA
    out, most = pl.pallas_call(
        kernel,
        out_shape=(
            jax.ShapeDtypeStruct((8, 256, 256), F32),
            jax.ShapeDtypeStruct((1, 1), jnp.int32),
        ),
        in_specs=[away] * 8,
        out_specs=(whole, whole),
        scratch_shapes=[
            pltpu.VMEM((4, 64, 1024), F32),
            pltpu.VMEM((8, 16, 1024), F32),
            pltpu.VMEM((1, 64), F32),
            pltpu.VMEM((1, 256), F32),
            pltpu.VMEM((1, 64), jnp.int32),
            pltpu.VMEM((1, 256), jnp.int32),
            pltpu.VMEM((1, 1024), jnp.int32),
            pltpu.VMEM((1, 1), jnp.int32),
            pltpu.VMEM((128, LANES), F32),
            pltpu.VMEM((128, LANES), F32),
            pltpu.VMEM((256, LANES), F32),
            pltpu.VMEM((256, LANES), F32),
            pltpu.VMEM((2, 12, 8, LANES), F32),
            pltpu.VMEM((2, 12, 8, LANES), F32),
            pltpu.VMEM((2, 8, 24, LANES), F32),
            pltpu.VMEM((8, 2, 24, LANES), F32),
            pltpu.VMEM((8, 2, 24, LANES), F32),
            pltpu.VMEM((12, 256, LANES), F32),
            pltpu.VMEM((8, 256, 256), F32),
            pltpu.VMEM((256, LANES), F32),
            pltpu.VMEM((256, LANES), F32),
            sems((8,)),
            sems((2,)),
            sems((2,)),
            sems((8,)),
            sems((8,)),
            sems((len(GATHER),)),
            sems((len(GATHER),)),
        ],
        compiler_params=pltpu.CompilerParams(collective_id=0, has_side_effects=True, vmem_limit_bytes=40 * 2**20),
        name="ladder",
    )(
        amplitudes,
        integrals,
        occ_energy.reshape(1, -1),
        vir_energy.reshape(1, -1),
        occ_irrep.reshape(1, -1),
        vir_irrep.reshape(1, -1),
        pair_irrep.reshape(1, -1),
        turn,
    )
    return out, most


def local(*args):
    turn = jnp.zeros((1, 1), jnp.int32)
    out, most = one_pass(turn, *args)

    def more(state):
        return (CAP * (state[0] + 1) < most)[0, 0]

    def step(state):
        turn = state[0] + 1
        return turn, state[1] + one_pass(turn, *args)[0]

    _, out = lax.while_loop(more, step, (turn, out))
    return jnp.transpose(out.reshape(8, 4, 64, 256), (1, 2, 0, 3))


def solution(mesh):
    placed = (P("occ", None, None), P("vir", "occ", None), P(), P(), P(), P(), P())
    return jax.shard_map(
        local, mesh=mesh, in_specs=placed, out_specs=P("occ", None, "vir", None), check_vma=False
    )
```

```python
import functools

import jax
import jax.numpy as jnp
from jax import lax
from jax.experimental import pallas as pl
from jax.experimental.pallas import tpu as pltpu
from jax.sharding import PartitionSpec as P

MESH = pl.DeviceIdType.MESH
F32 = jnp.float32
BF16 = jnp.bfloat16

LANES = 128
TAIL = 64
CAP = LANES + TAIL

OWN, XP, XM, X2 = (0, 0, 0), (1, 0, 0), (3, 0, 0), (2, 0, 0)
Z, ZP, ZM, Z2 = (0, 1, 0), (1, 1, 0), (3, 1, 0), (2, 1, 0)
CORE = (0, 0, 1)
CHIPS = (Z2, X2, ZP, ZM, XP, XM, Z)
ROUTES = (
    (OWN, ZP), (OWN, ZM), (OWN, X2), (OWN, Z), (OWN, XP), (OWN, XM), (OWN, CORE),
    (X2, Z), (X2, CORE),
    (Z, CORE), (XP, CORE), (XM, CORE), (ZM, CORE), (ZP, CORE), (Z2, CORE),
)


def gather_ops():
    ops, arrived = [], {}
    for whose, route in ROUTES:
        there = tuple((k - r) % n for k, r, n in zip(whose, route, (4, 2, 2)))
        after = arrived[whose] if whose != OWN else None
        arrived[there] = len(ops)
        ops.append((whose, route, after))
    return ops


GATHER = gather_ops()
LATE = 1


def split(x):
    high = x.astype(BF16)
    return high, (x - high.astype(F32)).astype(BF16)


def dot_t(a, b):
    return lax.dot_general(a, b, (((1,), (1,)), ((), ())), preferred_element_type=F32)


def at_lane(row, index):
    lane = lax.broadcasted_iota(jnp.int32, (index.shape[0], row.shape[1]), 1)
    return jnp.sum(jnp.where(lane == index, row, 0.0), axis=1, keepdims=True)


def iota_col(n):
    return lax.broadcasted_iota(jnp.int32, (n, 1), 0)


def kernel(
    t_hbm, v_hbm, eo_hbm, ev_hbm, so_hbm, sv_hbm, pair_hbm, turn_hbm, out_ref, most_ref,
    t_buf, v_buf, eo_ref, ev_ref, so_ref, sv_ref, pair_ref, turn_ref, vm, vt, tm, tt, t_send, t_recv, a_send, a_pair, a_recv,
    blocks, weight, a_main, a_tail, in_sem, ts_sem, tr_sem, as_sem, ar_sem, gs_sem, gr_sem,
):
    occ, vir = lax.axis_index("occ"), lax.axis_index("vir")
    x, zl, core = occ // 4, (occ // 2) % 2, occ % 2

    def member(step):
        return ((x + step[0]) % 4) * 4 + ((zl + step[1]) % 2) * 2 + (core + step[2]) % 2

    mirror_occ = vir // 2
    mirror_self = mirror_occ == occ
    bar = pltpu.get_barrier_semaphore()
    for h in range(2):

        @pl.when(jnp.logical_not(jnp.logical_and(mirror_self, vir % 2 == h)))
        def _():
            pl.semaphore_signal(bar, inc=1, device_id={"occ": mirror_occ, "vir": 2 * occ + h}, device_id_type=MESH)

    for step in CHIPS + (CORE,):
        pl.semaphore_signal(bar, inc=1, device_id={"occ": member(step)}, device_id_type=MESH)

    loads = [
        pltpu.make_async_copy(src, dst, in_sem.at[n])
        for n, (src, dst) in enumerate(
            (
                (pair_hbm, pair_ref), (turn_hbm, turn_ref), (sv_hbm, sv_ref), (v_hbm, v_buf),
                (so_hbm, so_ref), (t_hbm, t_buf), (eo_hbm, eo_ref), (ev_hbm, ev_ref),
            )
        )
    ]
    for load in loads:
        load.start()
    loads[0].wait()
    loads[1].wait()

    pair = pair_ref[...]
    hot = jnp.where(pair == lax.broadcasted_iota(jnp.int32, (8, pair.shape[1]), 0), 1.0, 0.0)
    upper = lax.broadcasted_iota(jnp.int32, (128, 128), 0) <= lax.broadcasted_iota(jnp.int32, (128, 128), 1)
    upper = jnp.where(upper, 1.0, 0.0).astype(BF16)
    parts = [hot[:, 128 * c : 128 * (c + 1)] for c in range(8)]
    counted = jnp.dot(jnp.concatenate(parts, axis=0).astype(BF16), upper, preferred_element_type=F32)
    before = jnp.zeros((8, 1), F32)
    ranks = []
    for c in range(8):
        here = counted[8 * c : 8 * (c + 1)]
        ranks.append(jnp.sum(parts[c] * (here + before), axis=0, keepdims=True))
        before = before + here[:, 127:128]
    rank = jnp.concatenate(ranks, axis=1) - 1.0 - CAP * turn_ref[...].astype(F32)
    most_ref[...] = jnp.broadcast_to(jnp.max(before, axis=0, keepdims=True), most_ref.shape).astype(jnp.int32)
    lane_of = iota_col(2 * LANES)
    lane_of = jnp.where(lane_of < CAP, lane_of, lane_of - TAIL).astype(F32)
    place = jnp.where(rank == lane_of, 1.0, 0.0).astype(BF16)

    first_half = lax.broadcasted_iota(jnp.int32, (1, LANES), 1) < TAIL

    def compact(values, sym):
        high, low = split(jnp.where(pair == sym, values, 0.0))
        return dot_t(high, place) + dot_t(low, place)

    loads[2].wait()
    sv_row = sv_ref[...].astype(F32)
    rows = iota_col(128)
    sym_v = at_lane(sv_row, 8 * vir + rows // 16).astype(jnp.int32) ^ at_lane(sv_row, 16 * occ + rows % 16).astype(jnp.int32)
    loads[3].wait()
    small = compact(v_buf[...].reshape(128, 1024), sym_v)
    vm[...] = small[:, :LANES]
    vt[...] = small[:, LANES:]
    for h in range(2):
        for q in range(4):
            for t in range(2):
                t_send[h, 3 * q + t] = vm[pl.ds(8 * h + q + 4 * t, 8, stride=16), :]
            t_send[h, 3 * q + 2] = jnp.where(
                first_half, vt[pl.ds(8 * h + q, 8, stride=16), :], vt[pl.ds(8 * h + q + 4, 8, stride=16), :]
            )

    @pl.when(mirror_self)
    def _():
        pl.semaphore_wait(bar, 9)

    @pl.when(jnp.logical_not(mirror_self))
    def _():
        pl.semaphore_wait(bar, 10)

    def mirror(h, slot):
        return pltpu.make_async_remote_copy(
            src_ref=t_send.at[h],
            dst_ref=t_recv.at[slot],
            send_sem=ts_sem.at[h],
            recv_sem=tr_sem.at[slot],
            device_id={"occ": mirror_occ, "vir": 2 * occ + h},
            device_id_type=MESH,
        )

    for h in range(2):
        to_self = jnp.logical_and(mirror_self, vir % 2 == h)

        @pl.when(to_self)
        def _():
            t_recv[h] = t_send[h]

        @pl.when(jnp.logical_not(to_self))
        def _():
            mirror(h, vir % 2).start()

    loads[4].wait()
    so_row = so_ref[...].astype(F32)
    rows = iota_col(256)
    sym_t = at_lane(so_row, 4 * occ + rows // 64).astype(jnp.int32) ^ at_lane(so_row, rows % 64).astype(jnp.int32)
    loads[5].wait()
    small = compact(t_buf[...].reshape(256, 1024), sym_t)
    tm[...] = small[:, :LANES]
    tt[...] = small[:, LANES:]
    packed = a_send.reshape(2 * 8 * 24, LANES)
    for i in range(4):
        for j in range(4):
            for c in range(2):
                packed[pl.ds(192 * c + 4 * i + j, 8, stride=24), :] = tm[pl.ds(64 * i + 4 * c + j, 8, stride=8), :]
        for j in range(2):
            for c in range(2):
                packed[pl.ds(192 * c + 16 + 2 * i + j, 8, stride=24), :] = jnp.where(
                    first_half,
                    tt[pl.ds(64 * i + 4 * c + j, 8, stride=8), :],
                    tt[pl.ds(64 * i + 4 * c + j + 2, 8, stride=8), :],
                )

    chip = occ // 2
    share = pltpu.make_async_remote_copy(
        src_ref=a_send.at[1 - core],
        dst_ref=a_pair.at[:, core],
        send_sem=as_sem.at[7],
        recv_sem=ar_sem.at[7],
        device_id={"occ": member(CORE)},
        device_id_type=MESH,
    )
    share.start()
    a_pair[:, core] = a_send[core]

    def swap(n, step):
        return pltpu.make_async_remote_copy(
            src_ref=a_pair.at[member(step) // 2],
            dst_ref=a_recv.at[chip],
            send_sem=as_sem.at[n],
            recv_sem=ar_sem.at[n],
            device_id={"occ": member(step)},
            device_id_type=MESH,
        )

    loads[6].wait()
    loads[7].wait()
    eo_row, ev_row = eo_ref[...], ev_ref[...]
    e_ij = at_lane(eo_row, 4 * occ + rows // 64) + at_lane(eo_row, rows % 64)
    sv_int = sv_ref[...]

    def weigh(a, carry):
        which = jnp.full((1, 1), 8 * vir + a, jnp.int32)
        sym_b = sv_int ^ at_lane(sv_row, which).astype(jnp.int32)
        e_b = at_lane(ev_row, which) + ev_row
        weight[a] = jnp.where(sym_t == sym_b, 1.0 / (e_ij - e_b), 0.0)
        return carry

    lax.fori_loop(0, 4, weigh, 0)
    share.wait_recv()
    swaps = [swap(n, step) for n, step in enumerate(CHIPS)]
    for copy in swaps:
        copy.start()
    a_recv[chip] = a_pair[chip]
    lax.fori_loop(4, 8, weigh, 0)

    mine = blocks.at[occ]
    for g in range(2):
        from_self = jnp.logical_and(mirror_self, vir % 2 == g)

        @pl.when(jnp.logical_not(from_self))
        def _():
            mirror(g, g).wait_recv()

        for q in range(4):
            for t in range(2):
                own = vm[pl.ds(16 * (q + 4 * t) + 8 * g, 8), :]
                mine[3 * q + t, pl.ds(8 * g, 8), :] = own - t_recv[g, 3 * q + t]
            own = jnp.where(first_half, vt[pl.ds(16 * q + 8 * g, 8), :], vt[pl.ds(16 * (q + 4) + 8 * g, 8), :])
            mine[3 * q + 2, pl.ds(8 * g, 8), :] = own - t_recv[g, 3 * q + 2]

    def hop(n, landing=False):
        whose, route, _ = GATHER[n]
        if landing:
            whose = tuple((k - r) % m for k, r, m in zip(whose, route, (4, 2, 2)))
        part = blocks.at[member(whose)]
        return pltpu.make_async_remote_copy(
            src_ref=part,
            dst_ref=part,
            send_sem=gs_sem.at[n],
            recv_sem=gr_sem.at[n],
            device_id={"occ": member(route)},
            device_id_type=MESH,
        )

    arrived = set()

    def need(n):
        if n not in arrived:
            arrived.add(n)
            hop(n, landing=True).wait_recv()

    for n, (_, _, after) in enumerate(GATHER):
        if after is None:
            hop(n).start()

    forwards = [n for n, (_, _, after) in enumerate(GATHER) if after is not None]
    for n in forwards[:LATE]:
        need(GATHER[n][2])
        hop(n).start()

    for copy in swaps:
        copy.wait_recv()
    theirs = a_recv.reshape(16 * 24, LANES)
    for i in range(4):
        for j in range(4):
            to = pl.ds(64 * i + j, 16, stride=4)
            a_main[to, :] = tm[to, :] - theirs[pl.ds(4 * j + i, 16, stride=24), :]
            tail = theirs[pl.ds(16 + 2 * j + i % 2, 16, stride=24), :]
            turned = pltpu.roll(tail, TAIL, 1)
            tail = jnp.where(first_half, tail, turned) if i < 2 else jnp.where(first_half, turned, tail)
            a_tail[to, :] = tt[to, :] - tail
    factors = []
    for t in range(2):
        kept = jnp.where(first_half if t == 0 else jnp.logical_not(first_half), a_tail[...], 0.0)
        high, low = split(jnp.concatenate([a_main[...], kept], axis=1))
        factors.append(jnp.concatenate([high, low, high], axis=1))

    for n in forwards[LATE:]:
        need(GATHER[n][2])
        hop(n).start()
    for n in range(len(GATHER)):
        need(n)

    def rows_of(n):
        return jnp.concatenate([blocks[o, n] for o in range(16)], axis=0)

    for q in range(4):
        for t in range(2):
            high, low = split(jnp.concatenate([rows_of(3 * q + t), rows_of(3 * q + 2)], axis=1))
            c = dot_t(factors[t], jnp.concatenate([high, high, low], axis=1))
            c = c * weight[q + 4 * t]
            for s in range(2):
                out_ref[s, pl.ds(q + 4 * t, 256, stride=8), :] = c[:, 128 * s : 128 * (s + 1)]
    for h in range(2):

        @pl.when(jnp.logical_not(jnp.logical_and(mirror_self, vir % 2 == h)))
        def _():
            mirror(h, vir % 2).wait_send()

    share.wait_send()
    for copy in swaps:
        copy.wait_send()
    for n in range(len(GATHER)):
        hop(n).wait_send()


def one_pass(turn, amplitudes, integrals, occ_energy, vir_energy, occ_irrep, vir_irrep, pair_irrep):
    whole = pl.BlockSpec(memory_space=pltpu.VMEM)
    away = pl.BlockSpec(memory_space=pl.ANY)
    sems = pltpu.SemaphoreType.DMA
    out, most = pl.pallas_call(
        kernel,
        out_shape=(
            jax.ShapeDtypeStruct((2, 2048, LANES), F32),
            jax.ShapeDtypeStruct((1, 1), jnp.int32),
        ),
        in_specs=[away] * 8,
        out_specs=(whole, whole),
        scratch_shapes=[
            pltpu.VMEM((4, 64, 1024), F32),
            pltpu.VMEM((8, 16, 1024), F32),
            pltpu.VMEM((1, 64), F32),
            pltpu.VMEM((1, 256), F32),
            pltpu.VMEM((1, 64), jnp.int32),
            pltpu.VMEM((1, 256), jnp.int32),
            pltpu.VMEM((1, 1024), jnp.int32),
            pltpu.VMEM((1, 1), jnp.int32),
            pltpu.VMEM((128, LANES), F32),
            pltpu.VMEM((128, LANES), F32),
            pltpu.VMEM((256, LANES), F32),
            pltpu.VMEM((256, LANES), F32),
            pltpu.VMEM((2, 12, 8, LANES), F32),
            pltpu.VMEM((2, 12, 8, LANES), F32),
            pltpu.VMEM((2, 8, 24, LANES), F32),
            pltpu.VMEM((8, 2, 24, LANES), F32),
            pltpu.VMEM((8, 2, 24, LANES), F32),
            pltpu.VMEM((16, 12, 16, LANES), F32),
            pltpu.VMEM((8, 256, 256), F32),
            pltpu.VMEM((256, LANES), F32),
            pltpu.VMEM((256, LANES), F32),
            sems((8,)),
            sems((2,)),
            sems((2,)),
            sems((8,)),
            sems((8,)),
            sems((len(GATHER),)),
            sems((len(GATHER),)),
        ],
        compiler_params=pltpu.CompilerParams(collective_id=0, has_side_effects=True, vmem_limit_bytes=40 * 2**20),
        name="ladder",
    )(
        amplitudes,
        integrals,
        occ_energy.reshape(1, -1),
        vir_energy.reshape(1, -1),
        occ_irrep.reshape(1, -1),
        vir_irrep.reshape(1, -1),
        pair_irrep.reshape(1, -1),
        turn,
    )
    return out, most


def place(src_ref, out_ref, sem):
    copies = [
        pltpu.make_async_copy(
            src_ref.at[s, i], out_ref.at[i, :, :, pl.ds(128 * s, 128)], sem.at[4 * s + i]
        )
        for s in range(2)
        for i in range(4)
    ]
    for copy in copies:
        copy.start()
    for copy in copies:
        copy.wait()


def lay_out(out):
    return pl.pallas_call(
        place,
        out_shape=jax.ShapeDtypeStruct((4, 64, 8, 256), F32),
        in_specs=[pl.BlockSpec(memory_space=pl.ANY)],
        out_specs=pl.BlockSpec(memory_space=pltpu.HBM),
        scratch_shapes=[pltpu.SemaphoreType.DMA((8,))],
        name="lay_out",
    )(out.reshape(2, 4, 64, 8, 128))


def local(*args):
    turn = jnp.zeros((1, 1), jnp.int32)
    out, most = one_pass(turn, *args)

    def more(state):
        return (CAP * (state[0] + 1) < most)[0, 0]

    def step(state):
        turn = state[0] + 1
        return turn, state[1] + one_pass(turn, *args)[0]

    _, out = lax.while_loop(more, step, (turn, out))
    return lay_out(out)


def solution(mesh):
    placed = (P("occ", None, None), P("vir", "occ", None), P(), P(), P(), P(), P())
    return jax.shard_map(
        local, mesh=mesh, in_specs=placed, out_specs=P("occ", None, "vir", None), check_vma=False
    )
```

```python
import functools

import jax
import jax.numpy as jnp
from jax import lax
from jax.experimental import pallas as pl
from jax.experimental.pallas import tpu as pltpu
from jax.sharding import PartitionSpec as P

MESH = pl.DeviceIdType.MESH
F32 = jnp.float32
BF16 = jnp.bfloat16

LANES = 128
TAIL = 32
CAP = LANES + TAIL
PER = LANES // TAIL
ROWS = 8 + 8 // PER

OWN, XP, XM, X2 = (0, 0, 0), (1, 0, 0), (3, 0, 0), (2, 0, 0)
Z, ZP, ZM, Z2 = (0, 1, 0), (1, 1, 0), (3, 1, 0), (2, 1, 0)
CORE = (0, 0, 1)
CHIPS = (Z2, X2, ZP, ZM, XP, XM, Z)
ROUTES = (
    (OWN, ZP), (OWN, ZM), (OWN, X2), (OWN, Z), (OWN, XP), (OWN, XM), (OWN, CORE),
    (X2, Z), (X2, CORE),
    (Z, CORE), (XP, CORE), (XM, CORE), (ZM, CORE), (ZP, CORE), (Z2, CORE),
)


def gather_ops():
    ops, arrived = [], {}
    for whose, route in ROUTES:
        there = tuple((k - r) % n for k, r, n in zip(whose, route, (4, 2, 2)))
        after = arrived[whose] if whose != OWN else None
        arrived[there] = len(ops)
        ops.append((whose, route, after))
    return ops


GATHER = gather_ops()
LATE = 1


def split(x):
    high = x.astype(BF16)
    return high, (x - high.astype(F32)).astype(BF16)


def dot_t(a, b):
    return lax.dot_general(a, b, (((1,), (1,)), ((), ())), preferred_element_type=F32)


def at_lane(row, index):
    lane = lax.broadcasted_iota(jnp.int32, (index.shape[0], row.shape[1]), 1)
    return jnp.sum(jnp.where(lane == index, row, 0.0), axis=1, keepdims=True)


def iota_col(n):
    return lax.broadcasted_iota(jnp.int32, (n, 1), 0)


def kernel(
    t_hbm, v_hbm, eo_hbm, ev_hbm, so_hbm, sv_hbm, pair_hbm, turn_hbm, out_ref, most_ref,
    t_buf, v_buf, eo_ref, ev_ref, so_ref, sv_ref, pair_ref, turn_ref, vm, vt, tm, tt, raw, raw_formed, t_send, t_recv, a_send, a_pair, a_recv,
    blocks, weight, a_main, a_tail, in_sem, raw_sem, ts_sem, tr_sem, as_sem, ar_sem, gs_sem, gr_sem,
):
    occ, vir = lax.axis_index("occ"), lax.axis_index("vir")
    x, zl, core = occ // 4, (occ // 2) % 2, occ % 2

    def member(step):
        return ((x + step[0]) % 4) * 4 + ((zl + step[1]) % 2) * 2 + (core + step[2]) % 2

    z_hi = vir // 8

    def block_of(step):
        return ((6 + 2 * z_hi - x - step[0]) % 4) * 4 + ((zl + step[1]) % 2) * 2 + (core + step[2]) % 2

    formed = block_of(OWN)
    moved = formed != occ
    mirror_occ = ((6 + 2 * x - z_hi) % 4) * 4 + (vir % 8) // 2

    bar = pltpu.get_barrier_semaphore()
    for g in range(2):
        pl.semaphore_signal(bar, inc=1, device_id={"occ": vir // 2, "vir": 2 * formed + g}, device_id_type=MESH)
    for step in CHIPS + (CORE,):
        pl.semaphore_signal(bar, inc=1, device_id={"occ": member(step)}, device_id_type=MESH)

    loads = [
        pltpu.make_async_copy(src, dst, in_sem.at[n])
        for n, (src, dst) in enumerate(
            (
                (pair_hbm, pair_ref), (turn_hbm, turn_ref), (sv_hbm, sv_ref), (v_hbm, v_buf),
                (so_hbm, so_ref), (t_hbm, t_buf), (eo_hbm, eo_ref), (ev_hbm, ev_ref),
            )
        )
    ]
    for load in loads:
        load.start()
    loads[0].wait()
    loads[1].wait()

    pair = pair_ref[...]
    hot = jnp.where(pair == lax.broadcasted_iota(jnp.int32, (8, pair.shape[1]), 0), 1.0, 0.0)
    upper = lax.broadcasted_iota(jnp.int32, (128, 128), 0) <= lax.broadcasted_iota(jnp.int32, (128, 128), 1)
    upper = jnp.where(upper, 1.0, 0.0).astype(BF16)
    parts = jnp.concatenate([hot[:, 128 * c : 128 * (c + 1)] for c in range(8)], axis=0)
    counted = jnp.dot(parts.astype(BF16), jnp.concatenate([upper, jnp.ones_like(upper)], axis=1), preferred_element_type=F32)
    run, of = lax.broadcasted_iota(jnp.int32, (64, 64), 0), lax.broadcasted_iota(jnp.int32, (64, 64), 1)
    earlier = jnp.where(jnp.logical_and(run % 8 == of % 8, of < run), 1.0, 0.0).astype(BF16)
    before = jnp.dot(earlier, counted[:, 128:].astype(BF16), preferred_element_type=F32)
    spots = parts * (counted[:, :128] + before)
    rank = jnp.concatenate([jnp.sum(spots[8 * c : 8 * (c + 1)], axis=0, keepdims=True) for c in range(8)], axis=1)
    rank = rank - 1.0 - CAP * turn_ref[...].astype(F32)
    total = (counted[56:, 128:] + before[56:])[:, :1]
    most_ref[...] = jnp.max(total, axis=0, keepdims=True).astype(jnp.int32)
    lane_of = iota_col(2 * LANES)
    lane_of = jnp.where(lane_of < LANES, lane_of, LANES + lane_of % TAIL).astype(F32)
    place = jnp.where(rank == lane_of, 1.0, 0.0).astype(BF16)

    lanes = lax.broadcasted_iota(jnp.int32, (1, LANES), 1)
    first_half = lanes < LANES // 2

    def side_by_side(tails):
        out = tails[0]
        for n in range(1, PER):
            out = jnp.where(lanes < n * TAIL, out, tails[n])
        return out

    def compact(values, sym):
        high, low = split(jnp.where(pair == sym, values, 0.0))
        both = dot_t(jnp.concatenate([high, low], axis=0), place)
        return both[: len(sym)] + both[len(sym) :]

    loads[2].wait()
    sv_row = sv_ref[...].astype(F32)
    rows = iota_col(128)
    sym_v = at_lane(sv_row, 8 * vir + rows // 16).astype(jnp.int32) ^ at_lane(sv_row, 16 * occ + rows % 16).astype(jnp.int32)
    loads[3].wait()
    small = compact(v_buf[...].reshape(128, 1024), sym_v)
    vm[...] = small[:, :LANES]
    vt[...] = small[:, LANES:]
    for h in range(2):
        for a in range(8):
            t_send[h, a] = vm[pl.ds(8 * h + a, 8, stride=16), :]
        for u in range(8 // PER):
            t_send[h, 8 + u] = side_by_side([vt[pl.ds(8 * h + PER * u + n, 8, stride=16), :] for n in range(PER)])

    pl.semaphore_wait(bar, len(CHIPS) + 3)

    def mirror(h, slot):
        return pltpu.make_async_remote_copy(
            src_ref=t_send.at[h],
            dst_ref=t_recv.at[slot],
            send_sem=ts_sem.at[h],
            recv_sem=tr_sem.at[slot],
            device_id={"occ": mirror_occ, "vir": 2 * occ + h},
            device_id_type=MESH,
        )

    for h in range(2):
        mirror(h, vir % 2).start()

    for a in range(8):
        raw[a] = vm[pl.ds(16 * a, 16), :]
    for u in range(8 // PER):
        raw[8 + u] = side_by_side([vt[pl.ds(16 * (PER * u + n), 16), :] for n in range(PER)])
    cross = pltpu.make_async_remote_copy(
        src_ref=raw,
        dst_ref=raw_formed,
        send_sem=raw_sem.at[0],
        recv_sem=raw_sem.at[1],
        device_id={"occ": formed},
        device_id_type=MESH,
    )

    @pl.when(moved)
    def _():
        cross.start()

    @pl.when(jnp.logical_not(moved))
    def _():
        raw_formed[...] = raw[...]

    loads[4].wait()
    so_row = so_ref[...].astype(F32)
    rows = iota_col(256)
    sym_t = at_lane(so_row, 4 * occ + rows // 64).astype(jnp.int32) ^ at_lane(so_row, rows % 64).astype(jnp.int32)
    loads[5].wait()
    small = compact(t_buf[...].reshape(256, 1024), sym_t)
    tm[...] = small[:, :LANES]
    tt[...] = small[:, LANES:]
    packed = a_send.reshape(2 * 8 * 24, LANES)
    for i in range(4):
        for j in range(4):
            for c in range(2):
                packed[pl.ds(192 * c + 4 * i + j, 8, stride=24), :] = tm[pl.ds(64 * i + 4 * c + j, 8, stride=8), :]
        for j in range(2):
            for c in range(2):
                packed[pl.ds(192 * c + 16 + 2 * i + j, 8, stride=24), :] = jnp.where(
                    first_half,
                    tt[pl.ds(64 * i + 4 * c + j, 8, stride=8), :],
                    tt[pl.ds(64 * i + 4 * c + j + 2, 8, stride=8), :],
                )

    chip = occ // 2
    share = pltpu.make_async_remote_copy(
        src_ref=a_send.at[1 - core],
        dst_ref=a_pair.at[:, core],
        send_sem=as_sem.at[7],
        recv_sem=ar_sem.at[7],
        device_id={"occ": member(CORE)},
        device_id_type=MESH,
    )
    share.start()
    a_pair[:, core] = a_send[core]

    def swap(n, step):
        return pltpu.make_async_remote_copy(
            src_ref=a_pair.at[member(step) // 2],
            dst_ref=a_recv.at[chip],
            send_sem=as_sem.at[n],
            recv_sem=ar_sem.at[n],
            device_id={"occ": member(step)},
            device_id_type=MESH,
        )

    loads[6].wait()
    loads[7].wait()
    eo_row, ev_row = eo_ref[...], ev_ref[...]
    e_ij = at_lane(eo_row, 4 * occ + rows // 64) + at_lane(eo_row, rows % 64)
    sv_int = sv_ref[...]

    def weigh(a, carry):
        which = jnp.full((1, 1), 8 * vir + a, jnp.int32)
        sym_b = sv_int ^ at_lane(sv_row, which).astype(jnp.int32)
        e_b = at_lane(ev_row, which) + ev_row
        denom = e_ij - e_b
        guess = pl.reciprocal(denom, approx=True)
        weight[a] = jnp.where(sym_t == sym_b, guess * (2.0 - denom * guess), 0.0)
        return carry

    lax.fori_loop(0, 4, weigh, 0)
    share.wait_recv()
    swaps = [swap(n, step) for n, step in enumerate(CHIPS)]
    for copy in swaps:
        copy.start()
    a_recv[chip] = a_pair[chip]
    lax.fori_loop(4, 8, weigh, 0)

    @pl.when(moved)
    def _():
        cross.wait_recv()

    for g in range(2):
        mirror(g, g).wait_recv()
        rows = pl.ds(8 * g, 8)
        blocks[formed, :, rows, :] = raw_formed[:, rows, :] - t_recv[g]

    def hop(n, landing=False):
        whose, route, _ = GATHER[n]
        if landing:
            whose = tuple((k - r) % m for k, r, m in zip(whose, route, (4, 2, 2)))
        part = blocks.at[block_of(whose)]
        return pltpu.make_async_remote_copy(
            src_ref=part,
            dst_ref=part,
            send_sem=gs_sem.at[n],
            recv_sem=gr_sem.at[n],
            device_id={"occ": member(route)},
            device_id_type=MESH,
        )

    arrived = set()

    def need(n):
        if n not in arrived:
            arrived.add(n)
            hop(n, landing=True).wait_recv()

    for n, (_, _, after) in enumerate(GATHER):
        if after is None:
            hop(n).start()

    forwards = [n for n, (_, _, after) in enumerate(GATHER) if after is not None]
    for n in forwards[:LATE]:
        need(GATHER[n][2])
        hop(n).start()

    for copy in swaps:
        copy.wait_recv()
    theirs = a_recv.reshape(16 * 24, LANES)
    for i in range(4):
        for j in range(4):
            to = pl.ds(64 * i + j, 16, stride=4)
            a_main[to, :] = tm[to, :] - theirs[pl.ds(4 * j + i, 16, stride=24), :]
            tail = theirs[pl.ds(16 + 2 * j + i % 2, 16, stride=24), :]
            turned = pltpu.roll(tail, LANES // 2, 1)
            tail = jnp.where(first_half, tail, turned) if i < 2 else jnp.where(first_half, turned, tail)
            a_tail[to, :] = tt[to, :] - tail
    factors = []
    for n in range(PER):
        kept = jnp.where(lanes // TAIL == n, a_tail[...], 0.0)
        high, low = split(jnp.concatenate([a_main[...], kept], axis=1))
        factors.append(jnp.concatenate([high, low, high], axis=1))

    for n in forwards[LATE:]:
        need(GATHER[n][2])
        hop(n).start()
    for n in range(len(GATHER)):
        need(n)

    def rows_of(n):
        return jnp.concatenate([blocks[o, n] for o in range(16)], axis=0)

    for a in range(8):
        high, low = split(jnp.concatenate([rows_of(a), rows_of(8 + a // PER)], axis=1))
        c = dot_t(factors[a % PER], jnp.concatenate([high, high, low], axis=1)) * weight[a]
        for s in range(2):
            out_ref[s, pl.ds(a, 256, stride=8), :] = c[:, 128 * s : 128 * (s + 1)]
    for h in range(2):
        mirror(h, vir % 2).wait_send()

    @pl.when(moved)
    def _():
        cross.wait_send()

    share.wait_send()
    for copy in swaps:
        copy.wait_send()
    for n in range(len(GATHER)):
        hop(n).wait_send()


def one_pass(turn, amplitudes, integrals, occ_energy, vir_energy, occ_irrep, vir_irrep, pair_irrep):
    whole = pl.BlockSpec(memory_space=pltpu.VMEM)
    away = pl.BlockSpec(memory_space=pl.ANY)
    sems = pltpu.SemaphoreType.DMA
    out, most = pl.pallas_call(
        kernel,
        out_shape=(
            jax.ShapeDtypeStruct((2, 2048, LANES), F32),
            jax.ShapeDtypeStruct((1, 1), jnp.int32),
        ),
        in_specs=[away] * 8,
        out_specs=(whole, whole),
        scratch_shapes=[
            pltpu.VMEM((4, 64, 1024), F32),
            pltpu.VMEM((8, 16, 1024), F32),
            pltpu.VMEM((1, 64), F32),
            pltpu.VMEM((1, 256), F32),
            pltpu.VMEM((1, 64), jnp.int32),
            pltpu.VMEM((1, 256), jnp.int32),
            pltpu.VMEM((1, 1024), jnp.int32),
            pltpu.VMEM((1, 1), jnp.int32),
            pltpu.VMEM((128, LANES), F32),
            pltpu.VMEM((128, LANES), F32),
            pltpu.VMEM((256, LANES), F32),
            pltpu.VMEM((256, LANES), F32),
            pltpu.VMEM((ROWS, 16, LANES), F32),
            pltpu.VMEM((ROWS, 16, LANES), F32),
            pltpu.VMEM((2, ROWS, 8, LANES), F32),
            pltpu.VMEM((2, ROWS, 8, LANES), F32),
            pltpu.VMEM((2, 8, 24, LANES), F32),
            pltpu.VMEM((8, 2, 24, LANES), F32),
            pltpu.VMEM((8, 2, 24, LANES), F32),
            pltpu.VMEM((16, ROWS, 16, LANES), F32),
            pltpu.VMEM((8, 256, 256), F32),
            pltpu.VMEM((256, LANES), F32),
            pltpu.VMEM((256, LANES), F32),
            sems((8,)),
            sems((2,)),
            sems((2,)),
            sems((2,)),
            sems((8,)),
            sems((8,)),
            sems((len(GATHER),)),
            sems((len(GATHER),)),
        ],
        compiler_params=pltpu.CompilerParams(collective_id=0, has_side_effects=True, vmem_limit_bytes=40 * 2**20),
        name="ladder",
    )(
        amplitudes,
        integrals,
        occ_energy.reshape(1, -1),
        vir_energy.reshape(1, -1),
        occ_irrep.reshape(1, -1),
        vir_irrep.reshape(1, -1),
        pair_irrep.reshape(1, -1),
        turn,
    )
    return out, most


def place(src_ref, out_ref, sem):
    copies = [
        pltpu.make_async_copy(
            src_ref.at[s, i], out_ref.at[i, :, :, pl.ds(128 * s, 128)], sem.at[4 * s + i]
        )
        for s in range(2)
        for i in range(4)
    ]
    for copy in copies:
        copy.start()
    for copy in copies:
        copy.wait()


def lay_out(out):
    return pl.pallas_call(
        place,
        out_shape=jax.ShapeDtypeStruct((4, 64, 8, 256), F32),
        in_specs=[pl.BlockSpec(memory_space=pl.ANY)],
        out_specs=pl.BlockSpec(memory_space=pltpu.HBM),
        scratch_shapes=[pltpu.SemaphoreType.DMA((8,))],
        name="lay_out",
    )(out.reshape(2, 4, 64, 8, 128))


def local(*args):
    turn = jnp.zeros((1, 1), jnp.int32)
    out, most = one_pass(turn, *args)

    def more(state):
        return (CAP * (state[0] + 1) < most)[0, 0]

    def step(state):
        turn = state[0] + 1
        return turn, state[1] + one_pass(turn, *args)[0]

    _, out = lax.while_loop(more, step, (turn, out))
    return lay_out(out)


def solution(mesh):
    placed = (P("occ", None, None), P("vir", "occ", None), P(), P(), P(), P(), P())
    return jax.shard_map(
        local, mesh=mesh, in_specs=placed, out_specs=P("occ", None, "vir", None), check_vma=False
    )
```

```python
import functools

import jax
import jax.numpy as jnp
from jax import lax
from jax.experimental import pallas as pl
from jax.experimental.pallas import tpu as pltpu
from jax.sharding import PartitionSpec as P

MESH = pl.DeviceIdType.MESH
F32 = jnp.float32
BF16 = jnp.bfloat16

LANES = 128
TAIL = 32
CAP = LANES + TAIL
PER = LANES // TAIL
ROWS = 8 + 8 // PER

OWN, XP, XM, X2 = (0, 0, 0), (1, 0, 0), (3, 0, 0), (2, 0, 0)
Z, ZP, ZM, Z2 = (0, 1, 0), (1, 1, 0), (3, 1, 0), (2, 1, 0)
CORE = (0, 0, 1)
CHIPS = (Z2, X2, ZP, ZM, XP, XM, Z)
ROUTES = (
    (OWN, X2), (OWN, ZP), (OWN, ZM), (OWN, Z), (OWN, XP), (OWN, XM), (OWN, CORE),
    (X2, Z),
    (Z, CORE), (XP, CORE), (XM, CORE), (X2, CORE), (ZM, CORE), (ZP, CORE), (Z2, CORE),
)


def gather_ops():
    ops, arrived = [], {}
    for whose, route in ROUTES:
        there = tuple((k - r) % n for k, r, n in zip(whose, route, (4, 2, 2)))
        after = arrived[whose] if whose != OWN else None
        arrived[there] = len(ops)
        ops.append((whose, route, after))
    return ops


GATHER = gather_ops()
LATE = 1


def split(x):
    high = x.astype(BF16)
    return high, (x - high.astype(F32)).astype(BF16)


def dot_t(a, b):
    return lax.dot_general(a, b, (((1,), (1,)), ((), ())), preferred_element_type=F32)


def at_lane(row, index):
    lane = lax.broadcasted_iota(jnp.int32, (index.shape[0], row.shape[1]), 1)
    return jnp.sum(jnp.where(lane == index, row, 0.0), axis=1, keepdims=True)


def iota_col(n):
    return lax.broadcasted_iota(jnp.int32, (n, 1), 0)


def kernel(
    t_hbm, v_hbm, eo_hbm, ev_hbm, so_hbm, sv_hbm, pair_hbm, turn_hbm, out_ref, most_ref,
    t_buf, v_buf, eo_ref, ev_ref, so_ref, sv_ref, pair_ref, turn_ref, vm, vt, tm, tt, raw, raw_formed, t_send, t_recv, a_send, a_pair, a_recv,
    blocks, weight, a_main, a_tail, in_sem, raw_sem, ts_sem, tr_sem, as_sem, ar_sem, gs_sem, gr_sem,
):
    occ, vir = lax.axis_index("occ"), lax.axis_index("vir")
    x, zl, core = occ // 4, (occ // 2) % 2, occ % 2

    def member(step):
        return ((x + step[0]) % 4) * 4 + ((zl + step[1]) % 2) * 2 + (core + step[2]) % 2

    z_hi = vir // 8

    def block_of(step):
        return ((6 + 2 * z_hi - x - step[0]) % 4) * 4 + ((zl + step[1]) % 2) * 2 + (core + step[2]) % 2

    formed = block_of(OWN)
    moved = formed != occ
    mirror_occ = ((6 + 2 * x - z_hi) % 4) * 4 + (vir % 8) // 2

    bar = pltpu.get_barrier_semaphore()
    for g in range(2):
        pl.semaphore_signal(bar, inc=1, device_id={"occ": vir // 2, "vir": 2 * formed + g}, device_id_type=MESH)
    for step in CHIPS + (CORE,):
        pl.semaphore_signal(bar, inc=1, device_id={"occ": member(step)}, device_id_type=MESH)

    loads = [
        pltpu.make_async_copy(src, dst, in_sem.at[n])
        for n, (src, dst) in enumerate(
            (
                (pair_hbm, pair_ref), (turn_hbm, turn_ref), (sv_hbm, sv_ref), (v_hbm, v_buf),
                (so_hbm, so_ref), (t_hbm, t_buf), (eo_hbm, eo_ref), (ev_hbm, ev_ref),
            )
        )
    ]
    for load in loads:
        load.start()
    loads[0].wait()
    loads[1].wait()

    pair = pair_ref[...]
    hot = jnp.where(pair == lax.broadcasted_iota(jnp.int32, (8, pair.shape[1]), 0), 1.0, 0.0)
    upper = lax.broadcasted_iota(jnp.int32, (128, 128), 0) <= lax.broadcasted_iota(jnp.int32, (128, 128), 1)
    upper = jnp.where(upper, 1.0, 0.0).astype(BF16)
    parts = jnp.concatenate([hot[:, 128 * c : 128 * (c + 1)] for c in range(8)], axis=0)
    counted = jnp.dot(parts.astype(BF16), jnp.concatenate([upper, jnp.ones_like(upper)], axis=1), preferred_element_type=F32)
    run, of = lax.broadcasted_iota(jnp.int32, (64, 64), 0), lax.broadcasted_iota(jnp.int32, (64, 64), 1)
    earlier = jnp.where(jnp.logical_and(run % 8 == of % 8, of < run), 1.0, 0.0).astype(BF16)
    before = jnp.dot(earlier, counted[:, 128:].astype(BF16), preferred_element_type=F32)
    spots = parts * (counted[:, :128] + before)
    rank = jnp.concatenate([jnp.sum(spots[8 * c : 8 * (c + 1)], axis=0, keepdims=True) for c in range(8)], axis=1)
    rank = rank - 1.0 - CAP * turn_ref[...].astype(F32)
    total = (counted[56:, 128:] + before[56:])[:, :1]
    most_ref[...] = jnp.max(total, axis=0, keepdims=True).astype(jnp.int32)
    lane_of = iota_col(2 * LANES)
    lane_of = jnp.where(lane_of < LANES, lane_of, LANES + lane_of % TAIL).astype(F32)
    place = jnp.where(rank == lane_of, 1.0, 0.0).astype(BF16)

    lanes = lax.broadcasted_iota(jnp.int32, (1, LANES), 1)
    first_half = lanes < LANES // 2

    def side_by_side(tails):
        out = tails[0]
        for n in range(1, PER):
            out = jnp.where(lanes < n * TAIL, out, tails[n])
        return out

    def compact(values, sym):
        high, low = split(jnp.where(pair == sym, values, 0.0))
        both = dot_t(jnp.concatenate([high, low], axis=0), place)
        return both[: len(sym)] + both[len(sym) :]

    loads[2].wait()
    sv_row = sv_ref[...].astype(F32)
    rows = iota_col(128)
    sym_v = at_lane(sv_row, 8 * vir + rows // 16).astype(jnp.int32) ^ at_lane(sv_row, 16 * occ + rows % 16).astype(jnp.int32)
    loads[3].wait()
    small = compact(v_buf[...].reshape(128, 1024), sym_v)
    vm[...] = small[:, :LANES]
    vt[...] = small[:, LANES:]
    for h in range(2):
        for a in range(8):
            t_send[h, a] = vm[pl.ds(8 * h + a, 8, stride=16), :]
        for u in range(8 // PER):
            t_send[h, 8 + u] = side_by_side([vt[pl.ds(8 * h + PER * u + n, 8, stride=16), :] for n in range(PER)])

    pl.semaphore_wait(bar, len(CHIPS) + 3)

    def mirror(h, slot):
        return pltpu.make_async_remote_copy(
            src_ref=t_send.at[h],
            dst_ref=t_recv.at[slot],
            send_sem=ts_sem.at[h],
            recv_sem=tr_sem.at[slot],
            device_id={"occ": mirror_occ, "vir": 2 * occ + h},
            device_id_type=MESH,
        )

    for h in range(2):
        mirror(h, vir % 2).start()

    for a in range(8):
        raw[a] = vm[pl.ds(16 * a, 16), :]
    for u in range(8 // PER):
        raw[8 + u] = side_by_side([vt[pl.ds(16 * (PER * u + n), 16), :] for n in range(PER)])
    cross = pltpu.make_async_remote_copy(
        src_ref=raw,
        dst_ref=raw_formed,
        send_sem=raw_sem.at[0],
        recv_sem=raw_sem.at[1],
        device_id={"occ": formed},
        device_id_type=MESH,
    )

    @pl.when(moved)
    def _():
        cross.start()

    @pl.when(jnp.logical_not(moved))
    def _():
        raw_formed[...] = raw[...]

    loads[4].wait()
    so_row = so_ref[...].astype(F32)
    rows = iota_col(256)
    sym_t = at_lane(so_row, 4 * occ + rows // 64).astype(jnp.int32) ^ at_lane(so_row, rows % 64).astype(jnp.int32)
    loads[5].wait()
    small = compact(t_buf[...].reshape(256, 1024), sym_t)
    tm[...] = small[:, :LANES]
    tt[...] = small[:, LANES:]
    packed = a_send.reshape(2 * 8 * 24, LANES)
    for i in range(4):
        for j in range(4):
            for c in range(2):
                packed[pl.ds(192 * c + 4 * i + j, 8, stride=24), :] = tm[pl.ds(64 * i + 4 * c + j, 8, stride=8), :]
        for j in range(2):
            for c in range(2):
                packed[pl.ds(192 * c + 16 + 2 * i + j, 8, stride=24), :] = jnp.where(
                    first_half,
                    tt[pl.ds(64 * i + 4 * c + j, 8, stride=8), :],
                    tt[pl.ds(64 * i + 4 * c + j + 2, 8, stride=8), :],
                )

    chip = occ // 2
    share = pltpu.make_async_remote_copy(
        src_ref=a_send.at[1 - core],
        dst_ref=a_pair.at[:, core],
        send_sem=as_sem.at[7],
        recv_sem=ar_sem.at[7],
        device_id={"occ": member(CORE)},
        device_id_type=MESH,
    )
    share.start()
    a_pair[:, core] = a_send[core]

    def swap(n, step):
        return pltpu.make_async_remote_copy(
            src_ref=a_pair.at[member(step) // 2],
            dst_ref=a_recv.at[chip],
            send_sem=as_sem.at[n],
            recv_sem=ar_sem.at[n],
            device_id={"occ": member(step)},
            device_id_type=MESH,
        )

    loads[6].wait()
    loads[7].wait()
    eo_row, ev_row = eo_ref[...], ev_ref[...]
    e_ij = at_lane(eo_row, 4 * occ + rows // 64) + at_lane(eo_row, rows % 64)
    sv_int = sv_ref[...]

    def weigh(a, carry):
        which = jnp.full((1, 1), 8 * vir + a, jnp.int32)
        sym_b = sv_int ^ at_lane(sv_row, which).astype(jnp.int32)
        e_b = at_lane(ev_row, which) + ev_row
        denom = e_ij - e_b
        guess = pl.reciprocal(denom, approx=True)
        weight[a] = jnp.where(sym_t == sym_b, guess * (2.0 - denom * guess), 0.0)
        return carry

    lax.fori_loop(0, 4, weigh, 0)
    share.wait_recv()
    swaps = [swap(n, step) for n, step in enumerate(CHIPS)]
    for copy in swaps:
        copy.start()
    a_recv[chip] = a_pair[chip]
    lax.fori_loop(4, 8, weigh, 0)

    @pl.when(moved)
    def _():
        cross.wait_recv()

    for g in range(2):
        mirror(g, g).wait_recv()
        rows = pl.ds(8 * g, 8)
        blocks[formed, :, rows, :] = raw_formed[:, rows, :] - t_recv[g]

    def hop(n, landing=False):
        whose, route, _ = GATHER[n]
        if landing:
            whose = tuple((k - r) % m for k, r, m in zip(whose, route, (4, 2, 2)))
        part = blocks.at[block_of(whose)]
        return pltpu.make_async_remote_copy(
            src_ref=part,
            dst_ref=part,
            send_sem=gs_sem.at[n],
            recv_sem=gr_sem.at[n],
            device_id={"occ": member(route)},
            device_id_type=MESH,
        )

    arrived = set()

    def need(n):
        if n not in arrived:
            arrived.add(n)
            hop(n, landing=True).wait_recv()

    for n, (_, _, after) in enumerate(GATHER):
        if after is None:
            hop(n).start()

    forwards = [n for n, (_, _, after) in enumerate(GATHER) if after is not None]
    for n in forwards[:LATE]:
        need(GATHER[n][2])
        hop(n).start()

    for copy in swaps:
        copy.wait_recv()
    theirs = a_recv.reshape(16 * 24, LANES)
    for i in range(4):
        for j in range(4):
            to = pl.ds(64 * i + j, 16, stride=4)
            a_main[to, :] = tm[to, :] - theirs[pl.ds(4 * j + i, 16, stride=24), :]
            tail = theirs[pl.ds(16 + 2 * j + i % 2, 16, stride=24), :]
            turned = pltpu.roll(tail, LANES // 2, 1)
            tail = jnp.where(first_half, tail, turned) if i < 2 else jnp.where(first_half, turned, tail)
            a_tail[to, :] = tt[to, :] - tail
    factors = []
    for n in range(PER):
        kept = jnp.where(lanes // TAIL == n, a_tail[...], 0.0)
        high, low = split(jnp.concatenate([a_main[...], kept], axis=1))
        factors.append(jnp.concatenate([high, low, high], axis=1))

    for n in forwards[LATE:]:
        need(GATHER[n][2])
        hop(n).start()
    for n in range(len(GATHER)):
        need(n)

    def rows_of(n):
        return jnp.concatenate([blocks[o, n] for o in range(16)], axis=0)

    for a in range(8):
        high, low = split(jnp.concatenate([rows_of(a), rows_of(8 + a // PER)], axis=1))
        c = dot_t(factors[a % PER], jnp.concatenate([high, high, low], axis=1)) * weight[a]
        for s in range(2):
            out_ref[s, pl.ds(a, 256, stride=8), :] = c[:, 128 * s : 128 * (s + 1)]
    for h in range(2):
        mirror(h, vir % 2).wait_send()

    @pl.when(moved)
    def _():
        cross.wait_send()

    share.wait_send()
    for copy in swaps:
        copy.wait_send()
    for n in range(len(GATHER)):
        hop(n).wait_send()


def one_pass(turn, amplitudes, integrals, occ_energy, vir_energy, occ_irrep, vir_irrep, pair_irrep):
    whole = pl.BlockSpec(memory_space=pltpu.VMEM)
    away = pl.BlockSpec(memory_space=pl.ANY)
    sems = pltpu.SemaphoreType.DMA
    out, most = pl.pallas_call(
        kernel,
        out_shape=(
            jax.ShapeDtypeStruct((2, 2048, LANES), F32),
            jax.ShapeDtypeStruct((1, 1), jnp.int32),
        ),
        in_specs=[away] * 8,
        out_specs=(whole, whole),
        scratch_shapes=[
            pltpu.VMEM((4, 64, 1024), F32),
            pltpu.VMEM((8, 16, 1024), F32),
            pltpu.VMEM((1, 64), F32),
            pltpu.VMEM((1, 256), F32),
            pltpu.VMEM((1, 64), jnp.int32),
            pltpu.VMEM((1, 256), jnp.int32),
            pltpu.VMEM((1, 1024), jnp.int32),
            pltpu.VMEM((1, 1), jnp.int32),
            pltpu.VMEM((128, LANES), F32),
            pltpu.VMEM((128, LANES), F32),
            pltpu.VMEM((256, LANES), F32),
            pltpu.VMEM((256, LANES), F32),
            pltpu.VMEM((ROWS, 16, LANES), F32),
            pltpu.VMEM((ROWS, 16, LANES), F32),
            pltpu.VMEM((2, ROWS, 8, LANES), F32),
            pltpu.VMEM((2, ROWS, 8, LANES), F32),
            pltpu.VMEM((2, 8, 24, LANES), F32),
            pltpu.VMEM((8, 2, 24, LANES), F32),
            pltpu.VMEM((8, 2, 24, LANES), F32),
            pltpu.VMEM((16, ROWS, 16, LANES), F32),
            pltpu.VMEM((8, 256, 256), F32),
            pltpu.VMEM((256, LANES), F32),
            pltpu.VMEM((256, LANES), F32),
            sems((8,)),
            sems((2,)),
            sems((2,)),
            sems((2,)),
            sems((8,)),
            sems((8,)),
            sems((len(GATHER),)),
            sems((len(GATHER),)),
        ],
        compiler_params=pltpu.CompilerParams(collective_id=0, has_side_effects=True, vmem_limit_bytes=40 * 2**20),
        name="ladder",
    )(
        amplitudes,
        integrals,
        occ_energy.reshape(1, -1),
        vir_energy.reshape(1, -1),
        occ_irrep.reshape(1, -1),
        vir_irrep.reshape(1, -1),
        pair_irrep.reshape(1, -1),
        turn,
    )
    return out, most


def place(src_ref, out_ref, sem):
    copies = [
        pltpu.make_async_copy(
            src_ref.at[s, i], out_ref.at[i, :, :, pl.ds(128 * s, 128)], sem.at[4 * s + i]
        )
        for s in range(2)
        for i in range(4)
    ]
    for copy in copies:
        copy.start()
    for copy in copies:
        copy.wait()


def lay_out(out):
    return pl.pallas_call(
        place,
        out_shape=jax.ShapeDtypeStruct((4, 64, 8, 256), F32),
        in_specs=[pl.BlockSpec(memory_space=pl.ANY)],
        out_specs=pl.BlockSpec(memory_space=pltpu.HBM),
        scratch_shapes=[pltpu.SemaphoreType.DMA((8,))],
        name="lay_out",
    )(out.reshape(2, 4, 64, 8, 128))


def local(*args):
    turn = jnp.zeros((1, 1), jnp.int32)
    out, most = one_pass(turn, *args)

    def more(state):
        return (CAP * (state[0] + 1) < most)[0, 0]

    def step(state):
        turn = state[0] + 1
        return turn, state[1] + one_pass(turn, *args)[0]

    _, out = lax.while_loop(more, step, (turn, out))
    return lay_out(out)


def solution(mesh):
    placed = (P("occ", None, None), P("vir", "occ", None), P(), P(), P(), P(), P())
    return jax.shard_map(
        local, mesh=mesh, in_specs=placed, out_specs=P("occ", None, "vir", None), check_vma=False
    )
```
